32 devices in a mesh: groups: 2 (over y), expert: 4 (over z), request: 4 (over x, core).
Axes of the slice: x: 2, y: 2, z: 4, core: 2. Of those that a mesh axis runs over, the one named last changes fastest.
Arguments:
- token_input: bfloat16 [2048, 4096], P(('groups', 'expert', 'request')), parts along dimension 0, may hold values from -6 to 6
- token_expert_index: int32 [2048, 8], P(('groups', 'expert', 'request')), parts along dimension 0, may hold values from 0 to 127, as said below
- token_request_index: int32 [2048], P(('groups', 'expert', 'request')), parts along dimension 0, may hold values from 0 to 15
- choice_weight: float32 [2048, 8], P(('groups', 'expert', 'request')), parts along dimension 0, may hold values from 0.05 to 1
- gate_weight: bfloat16 [4, 4096, 1024], P('expert', None, 'request'), may hold values from -0.09375 to 0.09375
- up_weight: bfloat16 [4, 4096, 1024], P('expert', None, 'request'), may hold values from -0.09375 to 0.09375
- down_weight: bfloat16 [4, 1024, 4096], P('expert', None, 'request'), may hold values from -0.1875 to 0.1875
- adapter_first_weight: bfloat16 [8, 16, 8, 1024], P(('groups', 'expert'), 'request'), parts along dimension 0, may hold values from -0.1875 to 0.1875
- adapter_second_weight: bfloat16 [8, 16, 8, 4096], P(('groups', 'expert'), 'request'), parts along dimension 0, may hold values from -2 to 2
Outputs:
- mixed: bfloat16 [2048, 4096], P(('groups', 'expert', 'request')), parts along dimension 0
The draws below stay inside these ranges and needn't reach their ends.
There are 2 independent parts, one for each index of `groups`. The reference program is written for one: setup_inputs(seed, part) draws one part's arguments, and reference() takes and returns one part's arrays. A program takes and returns all parts, laid end to end along the dimension named above; an argument that names none is the same for every part. Nothing has to cross between parts.
Inputs may be any that keep to these rules, and one draw needn't show every extreme that they name: `token_expert_index`: each row names 8 different experts. Within the 64 rows of one device each expert is named by no row or by exactly 4 rows.
All inputs are finite; a program needn't handle non-finite values.
Results may differ from the reference program's by a relative error of at most 0.0062.
Values may be sent and summed in bfloat16 or wider, within the bound.
No kernel may reach another device: no remote copies, remote signals or barrier semaphores. Data moves between devices by JAX's collectives and lax.ppermute only.
A program may use at most 64 MiB of HBM per device.

```python
import jax
import jax.numpy as jnp
from jax import lax

MODEL_WIDTH = 4096
ROUTED = 128
TOP = 8
EXPERT_HIDDEN = 1024
BATCH_REQUESTS = 16
ADAPTER_RANK = 8
CAP = 4
TOK_DEV = 64
LAYER_EXPERTS = 4
TOKENS = 1024


def route_plan(key):
    blocks = TOKENS // TOK_DEV
    groups_dev = TOK_DEV // CAP
    hotness = jax.random.randint(jax.random.fold_in(key, 71), (ROUTED,), 0, 4)
    noise = jax.random.randint(jax.random.fold_in(key, 72), (blocks, ROUTED), 0, 1024)
    scores = (noise + 512 * hotness[None, :]) * ROUTED + jnp.arange(ROUTED, dtype=jnp.int32)[None, :]
    ordering = jnp.argsort(-scores, axis=1).astype(jnp.int32)
    shuffle = jax.random.randint(jax.random.fold_in(key, 73), (blocks, TOP, TOK_DEV), 0, 4096)
    shuffle = shuffle * TOK_DEV + jnp.arange(TOK_DEV, dtype=jnp.int32)
    sigma = jnp.argsort(shuffle, axis=2).astype(jnp.int32)
    group_of = sigma // CAP
    spots = jnp.arange(TOP, dtype=jnp.int32)[None, :, None] * groups_dev + group_of
    chosen = jnp.take_along_axis(ordering, spots.reshape(blocks, TOP * TOK_DEV), axis=1)
    chosen = chosen.reshape(blocks, TOP, TOK_DEV)
    return jnp.transpose(chosen, (0, 2, 1)).reshape(TOKENS, TOP).astype(jnp.int32)


def draw_token_expert_index(key, part):
    return route_plan(key)


def touch_ends(drawn, key, low, largest):
    longest = drawn.shape.index(max(drawn.shape))
    spots = []
    for shift in (0, 1):
        where = [jax.random.randint(jax.random.fold_in(key, axis), (), 0, length) for axis, length in enumerate(drawn.shape)]
        where[longest] = (where[longest] + shift) % drawn.shape[longest]
        spots.append(tuple(where))
    return drawn.at[spots[0]].set(low).at[spots[1]].set(largest)


def level_of(stream_key, dims, pieces, low, top_value):
    level = 1.0
    for axis_at, shards_of in pieces:
        steps = jax.random.uniform(jax.random.fold_in(jax.random.fold_in(stream_key, 6), axis_at), (shards_of,), jnp.float32, low / len(pieces), top_value / len(pieces))
        level = level * jnp.repeat(jnp.exp(steps), dims[axis_at] // shards_of).reshape((-1,) + (1,) * (len(dims) - 1 - axis_at))
    return level


def scatter_about(rng, shape, deviation, most, cuts=(), held_as=jnp.bfloat16):
    factor_of = level_of(rng, shape, cuts, -0.22, 0.18) if cuts else 1.0
    entries = jax.random.normal(rng, shape, jnp.float32) * deviation * factor_of
    return jnp.minimum(jnp.maximum(entries, -most), most).astype(held_as)


def setup_inputs(seed: int = 0, part: int = 0) -> dict:
    key_of = jax.random.split(jax.random.key(seed), 10)
    own_keys = jax.random.split(jax.random.fold_in(key_of[9], part), 10)
    token_input = scatter_about(own_keys[0], (TOKENS, MODEL_WIDTH), 1.0, 6.0, ((0, 16),))
    token_expert_index = draw_token_expert_index(jax.random.fold_in(jax.random.fold_in(key_of[9], part), 71), part)
    token_request_index = touch_ends(jax.random.randint(own_keys[2], (TOKENS,), 0, BATCH_REQUESTS), jax.random.fold_in(own_keys[2], 1), 0, BATCH_REQUESTS - 1).astype(jnp.int32)
    choice_weight = jnp.clip(0.05 + 0.95 * jax.random.uniform(own_keys[3], (TOKENS, TOP), jnp.float32) ** level_of(own_keys[3], (TOKENS, TOP), ((0, 16),), -0.2, 0.2), 0.05, 1.0)
    gate_weight = scatter_about(key_of[4], (LAYER_EXPERTS, MODEL_WIDTH, EXPERT_HIDDEN), MODEL_WIDTH ** -0.5, 0.09375, ((0, 4), (2, 4)))
    up_weight = scatter_about(key_of[5], (LAYER_EXPERTS, MODEL_WIDTH, EXPERT_HIDDEN), MODEL_WIDTH ** -0.5, 0.09375, ((0, 4), (2, 4)))
    down_weight = scatter_about(key_of[6], (LAYER_EXPERTS, EXPERT_HIDDEN, MODEL_WIDTH), EXPERT_HIDDEN ** -0.5, 0.1875, ((0, 4), (2, 4)))
    adapter_first_weight = scatter_about(own_keys[7], (LAYER_EXPERTS, BATCH_REQUESTS, ADAPTER_RANK, EXPERT_HIDDEN), EXPERT_HIDDEN ** -0.5, 0.1875, ((0, 4), (1, 4)))
    adapter_second_weight = scatter_about(own_keys[8], (LAYER_EXPERTS, BATCH_REQUESTS, ADAPTER_RANK, MODEL_WIDTH), ADAPTER_RANK ** -0.5, 2.0, ((0, 4), (1, 4)))
    return dict(token_input=token_input, token_expert_index=token_expert_index, token_request_index=token_request_index, choice_weight=choice_weight, gate_weight=gate_weight, up_weight=up_weight, down_weight=down_weight, adapter_first_weight=adapter_first_weight, adapter_second_weight=adapter_second_weight)


def slot_rank(expert_ids):
    count = expert_ids.shape[-2]
    same = expert_ids[:, :, None, None] == expert_ids[None, None, :, :]
    earlier = jnp.arange(count, dtype=jnp.int32)[None, :] < jnp.arange(count, dtype=jnp.int32)[:, None]
    hits = jnp.logical_and(same, earlier[:, None, :, None]).astype(jnp.int32)
    return jnp.sum(hits, axis=(2, 3)).astype(jnp.int32)


def reference(token_input, token_expert_index, token_request_index, choice_weight, gate_weight, up_weight, down_weight, adapter_first_weight, adapter_second_weight):
    blocks = TOKENS // TOK_DEV
    per_expert = blocks * CAP
    spare = LAYER_EXPERTS * per_expert
    choice_slot_index = lax.map(slot_rank, token_expert_index.reshape(blocks, TOK_DEV, TOP)).reshape(TOKENS, TOP).astype(jnp.int32)
    token_index = jnp.arange(TOKENS, dtype=jnp.int32)
    block_index = (token_index // TOK_DEV)[:, None]
    position = (token_expert_index * blocks + block_index) * CAP + choice_slot_index
    position = jnp.where(token_expert_index < LAYER_EXPERTS, position, spare).reshape(-1).astype(jnp.int32)
    source = jnp.broadcast_to(token_index[:, None], token_expert_index.shape).reshape(-1)
    table_search = jnp.full((spare + 1,), TOKENS, jnp.int32).at[position].set(source)[:spare]
    table_search = table_search.reshape(LAYER_EXPERTS, per_expert)
    weight_arrays = jnp.zeros((spare + 1,), jnp.float32).at[position].set(choice_weight.reshape(-1))[:spare]
    weight_arrays = weight_arrays.reshape(LAYER_EXPERTS, per_expert)
    padded_in = jnp.concatenate([token_input, jnp.zeros((1, MODEL_WIDTH), token_input.dtype)], axis=0)
    padded_req = jnp.concatenate([token_request_index, jnp.full((1,), -1, jnp.int32)])
    column_holder = jnp.arange(BATCH_REQUESTS * ADAPTER_RANK, dtype=jnp.int32) // ADAPTER_RANK

    def expert_update(running_sums, inputs):
        lookup_row, weight_row, gate_w, up_w, down_w, first_f, second_f = inputs
        slot_rows = padded_in[lookup_row]
        slot_req = padded_req[lookup_row]
        gate_act = jnp.dot(slot_rows, gate_w, preferred_element_type=jnp.float32)
        up_act = jnp.dot(slot_rows, up_w, preferred_element_type=jnp.float32)
        hidden_units = (jax.nn.silu(gate_act) * up_act).astype(jnp.bfloat16)
        first_flat = first_f.reshape(BATCH_REQUESTS * ADAPTER_RANK, EXPERT_HIDDEN)
        reduced_rank_output = jnp.dot(hidden_units, first_flat.T, preferred_element_type=jnp.float32)
        selected = jnp.where(column_holder[None, :] == slot_req[:, None], reduced_rank_output, 0.0).astype(jnp.bfloat16)
        base = jnp.dot(hidden_units, down_w, preferred_element_type=jnp.float32)
        extra = jnp.dot(selected, second_f.reshape(BATCH_REQUESTS * ADAPTER_RANK, MODEL_WIDTH), preferred_element_type=jnp.float32)
        expert_out = (base + extra).astype(jnp.bfloat16)
        running_sums = running_sums.at[lookup_row].add(expert_out.astype(jnp.float32) * weight_row[:, None])
        return running_sums, None

    running_sums = jnp.zeros((TOKENS + 1, MODEL_WIDTH), jnp.float32)
    running_sums, unused_value = lax.scan(expert_update, running_sums, (table_search, weight_arrays, gate_weight, up_weight, down_weight, adapter_first_weight, adapter_second_weight))
    return running_sums[:TOKENS].astype(jnp.bfloat16)
```

```python
import functools

import jax
import jax.numpy as jnp
from jax import lax
from jax.experimental import pallas as pl
from jax.experimental.pallas import tpu as pltpu
from jax.sharding import PartitionSpec as P

CAP = 4
LANES = 128
VMEM = pl.BlockSpec(memory_space=pltpu.VMEM)


def xor_permute(value, axis, offset):
    return lax.ppermute(value, axis, [(i, i ^ offset) for i in range(lax.axis_size(axis))])


def slot_values(ids, values, expert):
    tokens = ids.shape[1]
    match = ids == expert
    named = jnp.sum(match.astype(jnp.float32), axis=0, keepdims=True)
    row = lax.broadcasted_iota(jnp.int32, (tokens, tokens), 0)
    col = lax.broadcasted_iota(jnp.int32, (tokens, tokens), 1)
    earlier = (row < col).astype(jnp.bfloat16)
    rank = jnp.dot(named.astype(jnp.bfloat16), earlier, preferred_element_type=jnp.float32)
    slot = lax.broadcasted_iota(jnp.int32, (CAP, tokens), 0).astype(jnp.float32)
    held = jnp.logical_and(slot == rank, named > 0)
    value = jnp.sum(jnp.where(match, values, 0.0), axis=0, keepdims=True)
    return jnp.where(held, value, 0.0)


def pack_kernel(ids_ref, req_ref, x_ref, *refs):
    out_refs, scratch = refs[:-1], refs[-1]
    experts = len(out_refs)
    me = lax.axis_index("expert")
    width = x_ref.shape[1]
    ids = ids_ref[...]
    ones = jnp.ones(ids.shape, jnp.float32)
    table = jnp.concatenate([slot_values(ids, ones, me ^ s) for s in range(experts)], axis=0)
    owner = jnp.sum(table * (req_ref[...] + 1).astype(jnp.float32), axis=1, keepdims=True) - 1.0
    scratch[:, :width] = jnp.dot(
        table.astype(jnp.bfloat16), x_ref[...], preferred_element_type=jnp.float32
    )
    scratch[:, width:] = jnp.broadcast_to(owner, (owner.shape[0], LANES))
    for s, out_ref in enumerate(out_refs):
        out_ref[...] = scratch[pl.ds(s * CAP, CAP), :].astype(out_ref.dtype)


def hidden_kernel(near_ref, far_ref, gate_ref, up_ref, hidden_ref, owner_ref):
    width = gate_ref.shape[1]
    rows = jnp.concatenate([near_ref[:, :width], far_ref[:, :width]], axis=0)
    gate = jnp.dot(rows, gate_ref[0], preferred_element_type=jnp.float32)
    up = jnp.dot(rows, up_ref[0], preferred_element_type=jnp.float32)
    hidden_ref[...] = (gate / (1.0 + jnp.exp(-gate)) * up).astype(hidden_ref.dtype)
    owner_ref[...] = jnp.concatenate([near_ref[:, width:], far_ref[:, width:]], axis=0)


def down_kernel(order, n_req, *refs):
    size = len(order)
    hid_refs = refs[:size]
    owner_ref, down_ref, first_ref, second_ref, out_ref, scratch = refs[size:]
    me_e, me_r = lax.axis_index("expert"), lax.axis_index("request")
    total, cols = scratch.shape
    block = total // size
    part = hid_refs[0].shape[1]
    columns = first_ref.shape[0]
    base = jnp.zeros((total, cols), jnp.float32)
    low = jnp.zeros((total, columns), jnp.float32)
    for s, hid_ref in enumerate(hid_refs):
        picks = [order.index(o ^ s) for o in order]
        hid = jnp.concatenate([hid_ref[j * block : (j + 1) * block, :] for j in picks], axis=0)
        at = pl.ds(pl.multiple_of((me_r ^ s) * part, part), part)
        base += jnp.dot(hid, down_ref[0, at, :], preferred_element_type=jnp.float32)
        low += lax.dot_general(
            hid, first_ref[:, at], (((1,), (1,)), ((), ())), preferred_element_type=jnp.float32
        )
    lane = lax.broadcasted_iota(jnp.int32, (1, columns), 1)
    per_dev = columns // size
    rank = per_dev // n_req
    holder = jnp.zeros((1, columns), jnp.int32)
    for i, o in enumerate(order):
        mine = (me_r ^ o) * n_req + (lane - i * per_dev) // rank
        holder = jnp.where(lane // per_dev == i, mine, holder)
    owner = owner_ref[:, :1].astype(jnp.int32)
    selected = jnp.where(holder == owner, low, 0.0).astype(jnp.bfloat16)
    scratch[...] = base + jnp.dot(selected, second_ref[...], preferred_element_type=jnp.float32)
    experts = block // CAP
    for i, o in enumerate(order):
        for s in range(experts):
            target = (me_e ^ s) * size + (me_r ^ o)
            rows = scratch[pl.ds(i * block + s * CAP, CAP), :]
            out_ref[target] = rows.astype(out_ref.dtype)


def combine_kernel(ids_ref, weight_ref, back_ref, mixed_ref, scratch):
    experts = scratch.shape[0] // CAP
    size = back_ref.shape[0] // experts
    cols = back_ref.shape[2]
    ids, weights = ids_ref[...], weight_ref[...]
    table = jnp.concatenate([slot_values(ids, weights, e) for e in range(experts)], axis=0)
    high = table.astype(jnp.bfloat16)
    rest = table - high.astype(jnp.float32)
    middle = rest.astype(jnp.bfloat16)
    low = (rest - middle.astype(jnp.float32)).astype(jnp.bfloat16)
    for r in range(size):
        for e in range(experts):
            scratch[pl.ds(e * CAP, CAP), :] = back_ref[e * size + r].astype(jnp.float32)
        rows = scratch[...].astype(jnp.bfloat16)
        mixed = sum(
            lax.dot_general(
                piece, rows, (((0,), (0,)), ((), ())), preferred_element_type=jnp.float32
            )
            for piece in (low, middle, high)
        )
        mixed_ref[:, r * cols : (r + 1) * cols] = mixed.astype(mixed_ref.dtype)


def body(
    token_input,
    token_expert_index,
    token_request_index,
    choice_weight,
    gate_weight,
    up_weight,
    down_weight,
    adapter_first_weight,
    adapter_second_weight,
):
    experts = lax.axis_size("expert")
    size = lax.axis_size("request")
    me_r = lax.axis_index("request")
    tokens, width = token_input.shape
    part = gate_weight.shape[2]
    cols = down_weight.shape[2]
    n_req, rank = adapter_first_weight.shape[1:3]
    bf16, f32 = jnp.bfloat16, jnp.float32
    params = pltpu.CompilerParams(vmem_limit_bytes=32 * 2**20)

    ids = token_expert_index.T
    weights = choice_weight.T
    packed = pl.pallas_call(
        pack_kernel,
        out_shape=[jax.ShapeDtypeStruct((CAP, width + LANES), bf16)] * experts,
        in_specs=[VMEM] * 3,
        out_specs=[VMEM] * experts,
        scratch_shapes=[pltpu.VMEM((experts * CAP, width + LANES), f32)],
        compiler_params=params,
    )(ids, token_request_index[None], token_input)

    first = adapter_first_weight.reshape(n_req * rank, -1)
    second = adapter_second_weight.reshape(n_req * rank, -1)
    rows = jnp.concatenate(
        [packed[0]] + [xor_permute(packed[s], "expert", s) for s in range(1, experts)], axis=0
    )
    order = [0]
    bit = size // 2
    near = far = rows
    while bit:
        half = second.shape[1] // 2
        upper = (me_r // bit) % 2
        keep = lax.dynamic_slice_in_dim(second, upper * half, half, 1)
        give = lax.dynamic_slice_in_dim(second, (1 - upper) * half, half, 1)
        second = jnp.concatenate([keep, xor_permute(give, "request", bit)], axis=0)
        first = jnp.concatenate([first, xor_permute(first, "request", bit)], axis=0)
        near = rows
        far = xor_permute(rows, "request", bit)
        order = order + [o ^ bit for o in order]
        bit //= 2
        if bit:
            rows = jnp.concatenate([near, far], axis=0)

    total = experts * CAP * size
    hidden, owner = pl.pallas_call(
        hidden_kernel,
        out_shape=[
            jax.ShapeDtypeStruct((total, part), bf16),
            jax.ShapeDtypeStruct((total, LANES), bf16),
        ],
        in_specs=[VMEM] * 4,
        out_specs=[VMEM] * 2,
        compiler_params=params,
    )(near, far, gate_weight, up_weight)

    shared = [hidden] + [xor_permute(hidden, "request", s) for s in range(1, size)]
    out = pl.pallas_call(
        functools.partial(down_kernel, order, n_req),
        out_shape=jax.ShapeDtypeStruct((experts * size, CAP, cols), bf16),
        in_specs=[VMEM] * (size + 4),
        out_specs=VMEM,
        scratch_shapes=[pltpu.VMEM((total, cols), f32)],
        compiler_params=params,
    )(*shared, owner, down_weight, first, second)

    back = lax.all_to_all(out, ("expert", "request"), 0, 0, tiled=True)
    return pl.pallas_call(
        combine_kernel,
        out_shape=jax.ShapeDtypeStruct((tokens, width), bf16),
        in_specs=[VMEM] * 3,
        out_specs=VMEM,
        scratch_shapes=[pltpu.VMEM((experts * CAP, cols), f32)],
        compiler_params=params,
    )(ids, weights, back)


def solution(mesh):
    in_specs = (
        P(("groups", "expert", "request"), None),
        P(("groups", "expert", "request"), None),
        P(("groups", "expert", "request")),
        P(("groups", "expert", "request"), None),
        P("expert", None, "request"),
        P("expert", None, "request"),
        P("expert", None, "request"),
        P(("groups", "expert"), "request", None, None),
        P(("groups", "expert"), "request", None, None),
    )
    out_specs = P(("groups", "expert", "request"), None)
    return jax.shard_map(body, mesh=mesh, in_specs=in_specs, out_specs=out_specs, check_vma=False)
```

```python
import functools

import jax
import jax.numpy as jnp
from jax import lax
from jax.experimental import pallas as pl
from jax.experimental.pallas import tpu as pltpu
from jax.sharding import Mesh, PartitionSpec as P

CAP = 4
LANES = 128
PAIR = 2
REQUEST = ("quad", "pair")
VMEM = pl.BlockSpec(memory_space=pltpu.VMEM)
HBM = pl.BlockSpec(memory_space=pltpu.HBM)
PARAMS = pltpu.CompilerParams(vmem_limit_bytes=16 * 2**20)


def xor_permute(value, axis, offset):
    return lax.ppermute(value, axis, [(i, i ^ offset) for i in range(lax.axis_size(axis))])


def slot_values(ids, values, expert):
    tokens = ids.shape[1]
    match = ids == expert
    named = jnp.sum(match.astype(jnp.float32), axis=0, keepdims=True)
    row = lax.broadcasted_iota(jnp.int32, (tokens, tokens), 0)
    col = lax.broadcasted_iota(jnp.int32, (tokens, tokens), 1)
    earlier = (row < col).astype(jnp.bfloat16)
    rank = jnp.dot(named.astype(jnp.bfloat16), earlier, preferred_element_type=jnp.float32)
    slot = lax.broadcasted_iota(jnp.int32, (CAP, tokens), 0).astype(jnp.float32)
    held = jnp.logical_and(slot == rank, named > 0)
    value = jnp.sum(jnp.where(match, values, 0.0), axis=0, keepdims=True)
    return jnp.where(held, value, 0.0)


def in_hbm(*values):
    return [pltpu.with_memory_space_constraint(v, pltpu.HBM) for v in values]


def copy_all(pairs, sems):
    copies = [pltpu.make_async_copy(a, b, sems.at[i]) for i, (a, b) in enumerate(pairs)]
    for copy in copies:
        copy.start()
    return copies


def pack_kernel(quads, ids_hbm, req_hbm, x_hbm, first_hbm, second_hbm, *refs):
    factor_refs, out_refs, scratches = refs[:quads], refs[quads:-5], refs[-5:]
    ids_ref, req_ref, x_ref, scratch, sems = scratches
    half = second_hbm.shape[1] // quads
    pairs = [(ids_hbm, ids_ref), (req_hbm, req_ref), (x_hbm, x_ref)]
    for q, factor_ref in enumerate(factor_refs):
        at = pl.multiple_of((lax.axis_index("quad") ^ q) * half, half)
        pairs.append((second_hbm.at[:, pl.ds(at, half)], factor_ref.at[:, pl.ds(0, half)]))
        pairs.append((first_hbm, factor_ref.at[:, pl.ds(half, first_hbm.shape[1])]))
    copies = copy_all(pairs, sems)
    experts = len(out_refs)
    me = lax.axis_index("expert")
    width = x_ref.shape[1]
    copies[0].wait()
    copies[1].wait()
    ids = ids_ref[...]
    ones = jnp.ones(ids.shape, jnp.float32)
    table = jnp.concatenate([slot_values(ids, ones, me ^ s) for s in range(experts)], axis=0)
    owner = jnp.sum(table * (req_ref[...] + 1).astype(jnp.float32), axis=1, keepdims=True) - 1.0
    scratch[:, width:] = jnp.broadcast_to(owner, (owner.shape[0], LANES))
    copies[2].wait()
    scratch[:, :width] = jnp.dot(
        table.astype(jnp.bfloat16), x_ref[...], preferred_element_type=jnp.float32
    )
    for s, out_ref in enumerate(out_refs):
        out_ref[...] = scratch[pl.ds(s * CAP, CAP), :].astype(out_ref.dtype)
    for copy in copies[3:]:
        copy.wait()


def stage_kernel(
    ids_hbm, weight_hbm, gate_hbm, up_hbm, down_hbm, after_ref,
    table_ref, own_ref, down_ref, ids_ref, weight_ref, sems,
):
    part = gate_hbm.shape[2]
    pairs = [
        (ids_hbm, ids_ref),
        (weight_hbm, weight_ref),
        (gate_hbm.at[0], own_ref.at[:, pl.ds(0, part)]),
        (up_hbm.at[0], own_ref.at[:, pl.ds(part, part)]),
        (down_hbm.at[0], down_ref),
    ]
    copies = copy_all(pairs, sems)
    copies[0].wait()
    copies[1].wait()
    ids, weights = ids_ref[...], weight_ref[...]
    experts = table_ref.shape[0] // (3 * CAP)
    table = jnp.concatenate([slot_values(ids, weights, e) for e in range(experts)], axis=0)
    high = table.astype(jnp.bfloat16)
    rest = table - high.astype(jnp.float32)
    middle = rest.astype(jnp.bfloat16)
    low = (rest - middle.astype(jnp.float32)).astype(jnp.bfloat16)
    table_ref[...] = jnp.concatenate([low, middle, high], axis=0)
    for copy in copies[2:]:
        copy.wait()


def hidden_kernel(near_ref, far_ref, own_ref, peer_ref, hidden_ref, owner_ref):
    width = near_ref.shape[1] - LANES
    part = own_ref.shape[1] // PAIR
    rows = jnp.concatenate([near_ref[:, :width], far_ref[:, :width]], axis=0)
    owner_ref[...] = jnp.concatenate([near_ref[:, width:], far_ref[:, width:]], axis=0)
    for b, ref in enumerate((own_ref, peer_ref)):
        both = jnp.dot(rows, ref[...], preferred_element_type=jnp.float32)
        gate, up = both[:, :part], both[:, part:]
        hidden = gate / (1.0 + jnp.exp(-gate)) * up
        hidden_ref[:, b * part : (b + 1) * part] = hidden.astype(hidden_ref.dtype)


def down_kernel(order, n_req, cols, *refs):
    quads = len(order)
    hid_refs, factor_refs = refs[:quads], refs[quads : 3 * quads]
    owner_ref, own_ref, peer_ref, out_ref, whole, scratch = refs[3 * quads :]
    me_e, me_q, me_p = (lax.axis_index(a) for a in ("expert", "quad", "pair"))
    me_r = me_q * PAIR + me_p
    total, depth = whole.shape
    block = total // quads
    part = hid_refs[0].shape[1] // PAIR
    for q, hid_ref in enumerate(hid_refs):
        picks = [order.index(o ^ q) for o in order]
        hid = jnp.concatenate([hid_ref[j * block : (j + 1) * block, :] for j in picks], axis=0)
        for b in range(PAIR):
            at = pl.multiple_of((me_r ^ (q * PAIR + b)) * part, part)
            whole[:, pl.ds(at, part)] = hid[:, b * part : (b + 1) * part]
    hidden = whole[...]
    owner = owner_ref[:, :1].astype(jnp.int32)
    per_dev = factor_refs[0].shape[0]
    rank = per_dev // n_req
    lane = lax.broadcasted_iota(jnp.int32, (1, per_dev * len(factor_refs)), 1)
    first = jnp.concatenate([ref[:, PAIR * cols :] for ref in factor_refs], axis=0)
    low = lax.dot_general(
        hidden, first, (((1,), (1,)), ((), ())), preferred_element_type=jnp.float32
    )
    holder = jnp.zeros_like(lane)
    for i in range(len(factor_refs)):
        mine = (me_r ^ i) * n_req + (lane - i * per_dev) // rank
        holder = jnp.where(lane // per_dev == i, mine, holder)
    chosen = jnp.where(holder == owner, low, 0.0).astype(jnp.bfloat16)
    for b, ref in enumerate((own_ref, peer_ref)):
        at = pl.ds(pl.multiple_of((me_p ^ b) * cols, cols), cols)
        second = jnp.concatenate([f[:, at] for f in factor_refs], axis=0)
        scratch[:, at] = jnp.dot(
            hidden, ref[...], preferred_element_type=jnp.float32
        ) + jnp.dot(chosen, second, preferred_element_type=jnp.float32)
    experts = block // CAP
    for i, o in enumerate(order):
        for s in range(experts):
            target = (me_e ^ s) * quads + (me_q ^ o)
            rows = scratch[pl.ds(i * block + s * CAP, CAP), :]
            out_ref[target] = rows.astype(out_ref.dtype)


def combine_kernel(table_ref, back_ref, mixed_hbm, scratch, done, sems):
    experts = scratch.shape[0] // CAP
    quads = done.shape[0]
    cols = done.shape[2]
    copies = []
    for q in range(quads):
        for e in range(experts):
            scratch[pl.ds(e * CAP, CAP), :] = back_ref[e * quads + q].astype(jnp.float32)
        rows = scratch[...].astype(jnp.bfloat16)
        mixed = lax.dot_general(
            table_ref[...], jnp.concatenate([rows] * 3, axis=0), (((0,), (0,)), ((), ())),
            preferred_element_type=jnp.float32,
        )
        done[q] = mixed.astype(done.dtype)
        at = pl.ds(q * cols, cols)
        copies.append(pltpu.make_async_copy(done.at[q], mixed_hbm.at[:, at], sems.at[q]))
        copies[-1].start()
    for copy in copies:
        copy.wait()


def body(
    token_input,
    token_expert_index,
    token_request_index,
    choice_weight,
    gate_weight,
    up_weight,
    down_weight,
    adapter_first_weight,
    adapter_second_weight,
):
    experts, quads = lax.axis_size("expert"), lax.axis_size("quad")
    tokens, width = token_input.shape
    part = gate_weight.shape[2]
    cols = down_weight.shape[2]
    n_req, rank, depth = adapter_first_weight.shape[1:]
    bf16, f32 = jnp.bfloat16, jnp.float32
    dma = pltpu.SemaphoreType.DMA
    own = n_req * rank

    ids = token_expert_index.T
    weights = choice_weight.T
    outs = pl.pallas_call(
        functools.partial(pack_kernel, quads),
        out_shape=[jax.ShapeDtypeStruct((own, width // quads + depth), bf16)] * quads
        + [jax.ShapeDtypeStruct((CAP, width + LANES), bf16)] * experts,
        in_specs=[HBM] * 5,
        out_specs=[VMEM] * (quads + experts),
        scratch_shapes=[
            pltpu.VMEM(ids.shape, jnp.int32),
            pltpu.VMEM((1, tokens), jnp.int32),
            pltpu.VMEM(token_input.shape, bf16),
            pltpu.VMEM((experts * CAP, width + LANES), f32),
            dma((3 + 2 * quads,)),
        ],
        compiler_params=PARAMS,
    )(
        *in_hbm(
            ids,
            token_request_index[None],
            token_input,
            adapter_first_weight.reshape(own, depth),
            adapter_second_weight.reshape(own, width),
        )
    )
    factors, packed = outs[:quads], outs[quads:]

    table, mine, down = pl.pallas_call(
        stage_kernel,
        out_shape=[
            jax.ShapeDtypeStruct((3 * experts * CAP, tokens), bf16),
            jax.ShapeDtypeStruct((width, PAIR * part), bf16),
            jax.ShapeDtypeStruct((depth, cols), bf16),
        ],
        in_specs=[HBM] * 5 + [VMEM],
        out_specs=[VMEM] * 3,
        scratch_shapes=[
            pltpu.VMEM(ids.shape, jnp.int32),
            pltpu.VMEM(weights.shape, f32),
            dma((5,)),
        ],
        compiler_params=PARAMS,
    )(*in_hbm(ids, weights, gate_weight, up_weight, down_weight), packed[0])

    blocks = [packed[0]] + [xor_permute(packed[s], "expert", s) for s in range(1, experts)]
    factors = [factors[0]] + [xor_permute(factors[q], REQUEST, q * PAIR) for q in range(1, quads)]
    mine, home = lax.optimization_barrier((mine, factors[0]))
    factors[0], peers = home, [xor_permute(home, REQUEST, 1)]
    blocks, mine, factors[1:] = lax.optimization_barrier((blocks, mine, factors[1:]))
    theirs = xor_permute(mine, REQUEST, 1)
    rows = jnp.concatenate(blocks, axis=0)
    rows, down, factors[1:] = lax.optimization_barrier((rows, down, factors[1:]))
    down2 = xor_permute(down, REQUEST, 1)
    peers += [xor_permute(f, REQUEST, 1) for f in factors[1:]]
    factors = [v for both in zip(factors, peers) for v in both]
    order = [0]
    bit = quads // 2
    while True:
        near = rows
        far = xor_permute(rows, REQUEST, bit * PAIR)
        order = order + [o ^ bit for o in order]
        bit //= 2
        if not bit:
            break
        rows = jnp.concatenate([near, far], axis=0)

    total = experts * CAP * quads
    hidden, owner = pl.pallas_call(
        hidden_kernel,
        out_shape=[
            jax.ShapeDtypeStruct((total, PAIR * part), bf16),
            jax.ShapeDtypeStruct((total, LANES), bf16),
        ],
        in_specs=[VMEM] * 4,
        out_specs=[VMEM] * 2,
        compiler_params=PARAMS,
    )(near, far, mine, theirs)

    shared = [hidden] + [xor_permute(hidden, REQUEST, q * PAIR) for q in range(1, quads)]
    out = pl.pallas_call(
        functools.partial(down_kernel, order, n_req, cols),
        out_shape=jax.ShapeDtypeStruct((experts * quads, CAP, PAIR * cols), bf16),
        in_specs=[VMEM] * (3 * quads + 3),
        out_specs=VMEM,
        scratch_shapes=[
            pltpu.VMEM((total, depth), bf16),
            pltpu.VMEM((total, PAIR * cols), f32),
        ],
        compiler_params=PARAMS,
    )(*shared, *factors, owner, down, down2)

    back = lax.all_to_all(out, ("expert", "quad"), 0, 0, tiled=True)
    return pl.pallas_call(
        combine_kernel,
        out_shape=jax.ShapeDtypeStruct((tokens, width), bf16),
        in_specs=[VMEM] * 2,
        out_specs=HBM,
        scratch_shapes=[
            pltpu.VMEM((experts * CAP, PAIR * cols), f32),
            pltpu.VMEM((quads, tokens, PAIR * cols), bf16),
            dma((quads,)),
        ],
        compiler_params=PARAMS,
    )(table, back)


def solution(mesh):
    groups, experts, requests = mesh.devices.shape
    fine = Mesh(
        mesh.devices.reshape(groups, experts, requests // PAIR, PAIR), ("groups", "expert", *REQUEST)
    )
    everyone = P(("groups", "expert", *REQUEST), None)
    weight = P("expert", None, REQUEST)
    adapter = P(("groups", "expert"), REQUEST, None, None)
    in_specs = (everyone, everyone, P(everyone[0]), everyone) + (weight,) * 3 + (adapter,) * 2
    return jax.shard_map(body, mesh=fine, in_specs=in_specs, out_specs=everyone, check_vma=False)
```

```python
import functools

import jax
import jax.numpy as jnp
from jax import lax
from jax.experimental import pallas as pl
from jax.experimental.pallas import tpu as pltpu
from jax.sharding import Mesh, PartitionSpec as P

CAP = 4
LANES = 128
PAIR = 2
REQUEST = ("quad", "pair")
VMEM = pl.BlockSpec(memory_space=pltpu.VMEM)
HBM = pl.BlockSpec(memory_space=pltpu.HBM)
PARAMS = pltpu.CompilerParams(vmem_limit_bytes=16 * 2**20)


def xor_permute(value, axis, offset):
    return lax.ppermute(value, axis, [(i, i ^ offset) for i in range(lax.axis_size(axis))])


def slot_values(ids, values, expert):
    tokens = ids.shape[1]
    match = ids == expert
    named = jnp.sum(match.astype(jnp.float32), axis=0, keepdims=True)
    row = lax.broadcasted_iota(jnp.int32, (tokens, tokens), 0)
    col = lax.broadcasted_iota(jnp.int32, (tokens, tokens), 1)
    earlier = (row < col).astype(jnp.bfloat16)
    rank = jnp.dot(named.astype(jnp.bfloat16), earlier, preferred_element_type=jnp.float32)
    slot = lax.broadcasted_iota(jnp.int32, (CAP, tokens), 0).astype(jnp.float32)
    held = jnp.logical_and(slot == rank, named > 0)
    value = jnp.sum(jnp.where(match, values, 0.0), axis=0, keepdims=True)
    return jnp.where(held, value, 0.0)


def in_hbm(*values):
    return [pltpu.with_memory_space_constraint(v, pltpu.HBM) for v in values]


def copy_all(pairs, sems):
    copies = [pltpu.make_async_copy(a, b, sems.at[i]) for i, (a, b) in enumerate(pairs)]
    for copy in copies:
        copy.start()
    return copies


def pack_kernel(
    quads, ids_hbm, req_hbm, x_hbm, first_hbm, second_hbm, gate_hbm, up_hbm, own_ref, *refs
):
    factor_refs, out_refs, scratches = refs[:quads], refs[quads:-5], refs[-5:]
    part = gate_hbm.shape[2]
    ids_ref, req_ref, x_ref, scratch, sems = scratches
    half = second_hbm.shape[1] // quads
    pairs = [(ids_hbm, ids_ref), (req_hbm, req_ref), (x_hbm, x_ref)]
    for q, factor_ref in enumerate(factor_refs):
        at = pl.multiple_of((lax.axis_index("quad") ^ q) * half, half)
        pairs.append((second_hbm.at[:, pl.ds(at, half)], factor_ref.at[:, pl.ds(0, half)]))
        pairs.append((first_hbm, factor_ref.at[:, pl.ds(half, first_hbm.shape[1])]))
    pairs.append((gate_hbm.at[0], own_ref.at[:, pl.ds(0, part)]))
    pairs.append((up_hbm.at[0], own_ref.at[:, pl.ds(part, part)]))
    copies = copy_all(pairs, sems)
    experts = len(out_refs)
    me = lax.axis_index("expert")
    width = x_ref.shape[1]
    copies[0].wait()
    copies[1].wait()
    ids = ids_ref[...]
    ones = jnp.ones(ids.shape, jnp.float32)
    table = jnp.concatenate([slot_values(ids, ones, me ^ s) for s in range(experts)], axis=0)
    owner = jnp.sum(table * (req_ref[...] + 1).astype(jnp.float32), axis=1, keepdims=True) - 1.0
    scratch[:, width:] = jnp.broadcast_to(owner, (owner.shape[0], LANES))
    copies[2].wait()
    scratch[:, :width] = jnp.dot(
        table.astype(jnp.bfloat16), x_ref[...], preferred_element_type=jnp.float32
    )
    for s, out_ref in enumerate(out_refs[::-1]):
        out_ref[...] = scratch[pl.ds(s * CAP, CAP), :].astype(out_ref.dtype)
    for copy in copies[3:]:
        copy.wait()


def stage_kernel(
    ids_hbm, weight_hbm, down_hbm, after_ref, table_ref, down_ref, ids_ref, weight_ref, sems
):
    pairs = [(ids_hbm, ids_ref), (weight_hbm, weight_ref), (down_hbm.at[0], down_ref)]
    copies = copy_all(pairs, sems)
    copies[0].wait()
    copies[1].wait()
    ids, weights = ids_ref[...], weight_ref[...]
    experts = table_ref.shape[0] // (3 * CAP)
    table = jnp.concatenate([slot_values(ids, weights, e) for e in range(experts)], axis=0)
    high = table.astype(jnp.bfloat16)
    rest = table - high.astype(jnp.float32)
    middle = rest.astype(jnp.bfloat16)
    low = (rest - middle.astype(jnp.float32)).astype(jnp.bfloat16)
    table_ref[...] = jnp.concatenate([low, middle, high], axis=0)
    for copy in copies[2:]:
        copy.wait()


def hidden_kernel(pieces, *refs):
    slot_refs, (own_ref, peer_ref, hidden_ref, owner_ref) = refs[:pieces], refs[pieces:]
    width = slot_refs[0].shape[1] - LANES
    part = own_ref.shape[1] // PAIR
    slots = jnp.concatenate([ref[...].astype(jnp.float32) for ref in slot_refs], axis=0)
    rows = slots[:, :width].astype(jnp.bfloat16)
    owner_ref[...] = slots[:, width:].astype(owner_ref.dtype)
    for b, ref in enumerate((own_ref, peer_ref)):
        both = jnp.dot(rows, ref[...], preferred_element_type=jnp.float32)
        gate, up = both[:, :part], both[:, part:]
        hidden = gate / (1.0 + jnp.exp(-gate)) * up
        hidden_ref[:, b * part : (b + 1) * part] = hidden.astype(hidden_ref.dtype)


def down_kernel(order, n_req, cols, *refs):
    quads = len(order)
    hid_refs, factor_refs = refs[:quads], refs[quads : quads + PAIR]
    owner_ref, own_ref, peer_ref, out_ref, whole, scratch = refs[quads + PAIR :]
    me_e, me_q, me_p = (lax.axis_index(a) for a in ("expert", "quad", "pair"))
    me_r = me_q * PAIR + me_p
    total, depth = whole.shape
    block = total // quads
    part = hid_refs[0].shape[1] // PAIR
    for q, hid_ref in enumerate(hid_refs):
        picks = [order.index(o ^ q) for o in order]
        hid = jnp.concatenate([hid_ref[j * block : (j + 1) * block, :] for j in picks], axis=0)
        for b in range(PAIR):
            at = pl.multiple_of((me_r ^ (q * PAIR + b)) * part, part)
            whole[:, pl.ds(at, part)] = hid[:, b * part : (b + 1) * part]
    hidden = whole[...]
    owner = owner_ref[:, :1].astype(jnp.int32)
    per_dev = factor_refs[0].shape[0] // quads
    rank = per_dev // n_req
    lane = lax.broadcasted_iota(jnp.int32, (1, per_dev * quads * PAIR), 1)
    first = jnp.concatenate([ref[:, PAIR * cols :] for ref in factor_refs], axis=0)
    low = lax.dot_general(
        hidden, first, (((1,), (1,)), ((), ())), preferred_element_type=jnp.float32
    )
    holder = jnp.zeros_like(lane)
    for i in range(quads * PAIR):
        holder_r = me_r ^ (i % quads * PAIR + i // quads)
        mine = holder_r * n_req + (lane - i * per_dev) // rank
        holder = jnp.where(lane // per_dev == i, mine, holder)
    chosen = jnp.where(holder == owner, low, 0.0).astype(jnp.bfloat16)
    for b, ref in enumerate((own_ref, peer_ref)):
        at = pl.ds(pl.multiple_of((me_p ^ b) * cols, cols), cols)
        second = jnp.concatenate([f[:, at] for f in factor_refs], axis=0)
        scratch[:, at] = jnp.dot(
            hidden, ref[...], preferred_element_type=jnp.float32
        ) + jnp.dot(chosen, second, preferred_element_type=jnp.float32)
    experts = block // CAP
    for i, o in enumerate(order):
        for s in range(experts):
            target = (me_e ^ s) * quads + (me_q ^ o)
            rows = scratch[pl.ds(i * block + s * CAP, CAP), :]
            out_ref[target] = rows.astype(out_ref.dtype)


def combine_kernel(table_ref, back_ref, mixed_hbm, scratch, done, sems):
    experts = scratch.shape[0] // CAP
    quads = done.shape[0]
    cols = done.shape[2]
    copies = []
    for q in range(quads):
        for e in range(experts):
            scratch[pl.ds(e * CAP, CAP), :] = back_ref[e * quads + q].astype(jnp.float32)
        rows = scratch[...].astype(jnp.bfloat16)
        mixed = lax.dot_general(
            table_ref[...], jnp.concatenate([rows] * 3, axis=0), (((0,), (0,)), ((), ())),
            preferred_element_type=jnp.float32,
        )
        done[q] = mixed.astype(done.dtype)
        at = pl.ds(q * cols, cols)
        copies.append(pltpu.make_async_copy(done.at[q], mixed_hbm.at[:, at], sems.at[q]))
        copies[-1].start()
    for copy in copies:
        copy.wait()


def body(
    token_input,
    token_expert_index,
    token_request_index,
    choice_weight,
    gate_weight,
    up_weight,
    down_weight,
    adapter_first_weight,
    adapter_second_weight,
):
    experts, quads = lax.axis_size("expert"), lax.axis_size("quad")
    tokens, width = token_input.shape
    part = gate_weight.shape[2]
    cols = down_weight.shape[2]
    n_req, rank, depth = adapter_first_weight.shape[1:]
    bf16, f32 = jnp.bfloat16, jnp.float32
    dma = pltpu.SemaphoreType.DMA
    own = n_req * rank

    ids = token_expert_index.T
    weights = choice_weight.T
    mine, *outs = pl.pallas_call(
        functools.partial(pack_kernel, quads),
        out_shape=[jax.ShapeDtypeStruct((width, PAIR * part), bf16)]
        + [jax.ShapeDtypeStruct((own, width // quads + depth), bf16)] * quads
        + [jax.ShapeDtypeStruct((CAP, width + LANES), bf16)] * experts,
        in_specs=[HBM] * 7,
        out_specs=[VMEM] * (1 + quads + experts),
        scratch_shapes=[
            pltpu.VMEM(ids.shape, jnp.int32),
            pltpu.VMEM((1, tokens), jnp.int32),
            pltpu.VMEM(token_input.shape, bf16),
            pltpu.VMEM((experts * CAP, width + LANES), f32),
            dma((5 + 2 * quads,)),
        ],
        compiler_params=PARAMS,
    )(
        *in_hbm(
            ids,
            token_request_index[None],
            token_input,
            adapter_first_weight.reshape(own, depth),
            adapter_second_weight.reshape(own, width),
            gate_weight,
            up_weight,
        )
    )
    theirs = xor_permute(mine, REQUEST, 1)
    factors, packed = outs[:quads], outs[quads:][::-1]

    blocks = [xor_permute(packed[s], "expert", s) for s in reversed(range(1, experts))]
    blocks = [packed[0]] + blocks[::-1]
    table, down = pl.pallas_call(
        stage_kernel,
        out_shape=[
            jax.ShapeDtypeStruct((3 * experts * CAP, tokens), bf16),
            jax.ShapeDtypeStruct((depth, cols), bf16),
        ],
        in_specs=[HBM] * 3 + [VMEM],
        out_specs=[VMEM] * 2,
        scratch_shapes=[
            pltpu.VMEM(ids.shape, jnp.int32),
            pltpu.VMEM(weights.shape, f32),
            dma((3,)),
        ],
        compiler_params=PARAMS,
    )(*in_hbm(ids, weights, down_weight), packed[0])

    factors = [factors[0]] + [xor_permute(factors[q], REQUEST, q * PAIR) for q in range(1, quads)]
    blocks, down, factors[1:] = lax.optimization_barrier((blocks[::-1], down, factors[1:]))
    blocks = blocks[::-1]
    rows = jnp.concatenate(blocks, axis=0)
    order, bit, slots = [0], quads // 2, []
    while bit:
        far = xor_permute(rows, REQUEST, bit * PAIR)
        order = order + [o ^ bit for o in order]
        bit //= 2
        slots = [rows, far]
        rows = jnp.concatenate(slots, axis=0) if bit else rows

    factors = jnp.concatenate(factors, axis=0)
    slots, down, factors = lax.optimization_barrier((slots, down, factors))
    down2 = xor_permute(down, REQUEST, 1)
    factors = (factors, xor_permute(factors, REQUEST, 1))

    total = experts * CAP * quads
    hidden, owner = pl.pallas_call(
        functools.partial(hidden_kernel, len(slots)),
        out_shape=[
            jax.ShapeDtypeStruct((total, PAIR * part), bf16),
            jax.ShapeDtypeStruct((total, LANES), bf16),
        ],
        in_specs=[VMEM] * (len(slots) + 2),
        out_specs=[VMEM] * 2,
        compiler_params=PARAMS,
    )(*slots, mine, theirs)

    shared = [hidden] + [xor_permute(hidden, REQUEST, q * PAIR) for q in range(1, quads)]
    out = pl.pallas_call(
        functools.partial(down_kernel, order, n_req, cols),
        out_shape=jax.ShapeDtypeStruct((experts * quads, CAP, PAIR * cols), bf16),
        in_specs=[VMEM] * (quads + PAIR + 3),
        out_specs=VMEM,
        scratch_shapes=[
            pltpu.VMEM((total, depth), bf16),
            pltpu.VMEM((total, PAIR * cols), f32),
        ],
        compiler_params=PARAMS,
    )(*shared, *factors, owner, down, down2)

    back = lax.all_to_all(out, ("expert", "quad"), 0, 0, tiled=True)
    return pl.pallas_call(
        combine_kernel,
        out_shape=jax.ShapeDtypeStruct((tokens, width), bf16),
        in_specs=[VMEM] * 2,
        out_specs=HBM,
        scratch_shapes=[
            pltpu.VMEM((experts * CAP, PAIR * cols), f32),
            pltpu.VMEM((quads, tokens, PAIR * cols), bf16),
            dma((quads,)),
        ],
        compiler_params=PARAMS,
    )(table, back)


def solution(mesh):
    groups, experts, requests = mesh.devices.shape
    fine = Mesh(
        mesh.devices.reshape(groups, experts, requests // PAIR, PAIR), ("groups", "expert", *REQUEST)
    )
    everyone = P(("groups", "expert", *REQUEST), None)
    weight = P("expert", None, REQUEST)
    adapter = P(("groups", "expert"), REQUEST, None, None)
    in_specs = (everyone, everyone, P(everyone[0]), everyone) + (weight,) * 3 + (adapter,) * 2
    return jax.shard_map(body, mesh=fine, in_specs=in_specs, out_specs=everyone, check_vma=False)
```

```python
import functools

import jax
import jax.numpy as jnp
from jax import lax
from jax.experimental import pallas as pl
from jax.experimental.pallas import tpu as pltpu
from jax.sharding import Mesh, PartitionSpec as P

CAP = 4
LANES = 128
PAIR = 2
REQUEST = ("quad", "pair")
VMEM = pl.BlockSpec(memory_space=pltpu.VMEM)
HBM = pl.BlockSpec(memory_space=pltpu.HBM)
PARAMS = pltpu.CompilerParams(vmem_limit_bytes=16 * 2**20)


def xor_permute(value, axis, offset):
    return lax.ppermute(value, axis, [(i, i ^ offset) for i in range(lax.axis_size(axis))])


def slot_values(ids, values, expert):
    tokens = ids.shape[1]
    match = ids == expert
    named = jnp.sum(match.astype(jnp.float32), axis=0, keepdims=True)
    row = lax.broadcasted_iota(jnp.int32, (tokens, tokens), 0)
    col = lax.broadcasted_iota(jnp.int32, (tokens, tokens), 1)
    earlier = (row < col).astype(jnp.bfloat16)
    rank = jnp.dot(named.astype(jnp.bfloat16), earlier, preferred_element_type=jnp.float32)
    slot = lax.broadcasted_iota(jnp.int32, (CAP, tokens), 0).astype(jnp.float32)
    held = jnp.logical_and(slot == rank, named > 0)
    value = jnp.sum(jnp.where(match, values, 0.0), axis=0, keepdims=True)
    return jnp.where(held, value, 0.0)


def in_hbm(*values):
    return [pltpu.with_memory_space_constraint(v, pltpu.HBM) for v in values]


def copy_all(pairs, sems):
    copies = [pltpu.make_async_copy(a, b, sems.at[i]) for i, (a, b) in enumerate(pairs)]
    for copy in copies:
        copy.start()
    return copies


def pack_kernel(
    quads, ids_hbm, req_hbm, x_hbm, first_hbm, second_hbm, *refs
):
    factor_refs, out_refs, scratches = refs[:quads], refs[quads:-5], refs[-5:]
    ids_ref, req_ref, x_ref, scratch, sems = scratches
    half = second_hbm.shape[1] // quads
    pairs = [(ids_hbm, ids_ref), (req_hbm, req_ref), (x_hbm, x_ref)]
    for q, factor_ref in enumerate(factor_refs):
        at = pl.multiple_of((lax.axis_index("quad") ^ q) * half, half)
        pairs.append((second_hbm.at[:, pl.ds(at, half)], factor_ref.at[:, pl.ds(0, half)]))
        pairs.append((first_hbm, factor_ref.at[:, pl.ds(half, first_hbm.shape[1])]))
    copies = copy_all(pairs, sems)
    experts = len(out_refs)
    me = lax.axis_index("expert")
    width = x_ref.shape[1]
    copies[0].wait()
    copies[1].wait()
    ids = ids_ref[...]
    ones = jnp.ones(ids.shape, jnp.float32)
    table = jnp.concatenate([slot_values(ids, ones, me ^ s) for s in range(experts)], axis=0)
    owner = jnp.sum(table * (req_ref[...] + 1).astype(jnp.float32), axis=1, keepdims=True) - 1.0
    scratch[:, width:] = jnp.broadcast_to(owner, (owner.shape[0], LANES))
    copies[2].wait()
    scratch[:, :width] = jnp.dot(
        table.astype(jnp.bfloat16), x_ref[...], preferred_element_type=jnp.float32
    )
    for s, out_ref in enumerate(out_refs[::-1]):
        out_ref[...] = scratch[pl.ds(s * CAP, CAP), :].astype(out_ref.dtype)
    for copy in copies[3:]:
        copy.wait()


def stage_kernel(
    ids_hbm, weight_hbm, up_hbm, after_ref, table_ref, up_ref, ids_ref, weight_ref, sems
):
    pairs = [(ids_hbm, ids_ref), (weight_hbm, weight_ref), (up_hbm, up_ref)]
    copies = copy_all(pairs, sems)
    copies[0].wait()
    copies[1].wait()
    ids, weights = ids_ref[...], weight_ref[...]
    experts = table_ref.shape[0] // (3 * CAP)
    table = jnp.concatenate([slot_values(ids, weights, e) for e in range(experts)], axis=0)
    high = table.astype(jnp.bfloat16)
    rest = table - high.astype(jnp.float32)
    middle = rest.astype(jnp.bfloat16)
    low = (rest - middle.astype(jnp.float32)).astype(jnp.bfloat16)
    table_ref[...] = jnp.concatenate([low, middle, high], axis=0)
    for copy in copies[2:]:
        copy.wait()


def hidden_kernel(pieces, *refs):
    slot_refs, refs = refs[:pieces], refs[pieces:]
    gate_ref, up_ref, gate2_ref, up2_ref, hidden_ref, owner_ref = refs
    width, part = gate_ref.shape[1:]
    slots = jnp.concatenate([ref[...].astype(jnp.float32) for ref in slot_refs], axis=0)
    rows = slots[:, :width].astype(jnp.bfloat16)
    owner_ref[...] = slots[:, width:].astype(owner_ref.dtype)
    for b, (g_ref, u_ref) in enumerate(((gate_ref, up_ref), (gate2_ref, up2_ref))):
        gate = jnp.dot(rows, g_ref[0], preferred_element_type=jnp.float32)
        up = jnp.dot(rows, u_ref[0], preferred_element_type=jnp.float32)
        hidden = gate / (1.0 + jnp.exp(-gate)) * up
        hidden_ref[:, b * part : (b + 1) * part] = hidden.astype(hidden_ref.dtype)


def down_kernel(order, n_req, cols, *refs):
    quads = len(order)
    hid_refs, factor_refs = refs[:quads], refs[quads : quads + PAIR]
    owner_ref, own_ref, peer_ref, out_ref, whole, scratch = refs[quads + PAIR :]
    me_e, me_q, me_p = (lax.axis_index(a) for a in ("expert", "quad", "pair"))
    me_r = me_q * PAIR + me_p
    total, depth = whole.shape
    block = total // quads
    part = hid_refs[0].shape[1] // PAIR
    for q, hid_ref in enumerate(hid_refs):
        picks = [order.index(o ^ q) for o in order]
        hid = jnp.concatenate([hid_ref[j * block : (j + 1) * block, :] for j in picks], axis=0)
        for b in range(PAIR):
            at = pl.multiple_of((me_r ^ (q * PAIR + b)) * part, part)
            whole[:, pl.ds(at, part)] = hid[:, b * part : (b + 1) * part]
    hidden = whole[...]
    owner = owner_ref[:, :1].astype(jnp.int32)
    per_dev = factor_refs[0].shape[0] // quads
    rank = per_dev // n_req
    lane = lax.broadcasted_iota(jnp.int32, (1, per_dev * quads * PAIR), 1)
    first = jnp.concatenate([ref[:, PAIR * cols :] for ref in factor_refs], axis=0)
    low = lax.dot_general(
        hidden, first, (((1,), (1,)), ((), ())), preferred_element_type=jnp.float32
    )
    holder = jnp.zeros_like(lane)
    for i in range(quads * PAIR):
        holder_r = me_r ^ (i % quads * PAIR + i // quads)
        mine = holder_r * n_req + (lane - i * per_dev) // rank
        holder = jnp.where(lane // per_dev == i, mine, holder)
    chosen = jnp.where(holder == owner, low, 0.0).astype(jnp.bfloat16)
    for b, ref in enumerate((own_ref, peer_ref)):
        at = pl.ds(pl.multiple_of((me_p ^ b) * cols, cols), cols)
        second = jnp.concatenate([f[:, at] for f in factor_refs], axis=0)
        scratch[:, at] = jnp.dot(
            hidden, ref[...], preferred_element_type=jnp.float32
        ) + jnp.dot(chosen, second, preferred_element_type=jnp.float32)
    experts = block // CAP
    for i, o in enumerate(order):
        for s in range(experts):
            target = (me_e ^ s) * quads + (me_q ^ o)
            rows = scratch[pl.ds(i * block + s * CAP, CAP), :]
            out_ref[target] = rows.astype(out_ref.dtype)


def combine_kernel(table_ref, back_ref, mixed_hbm, scratch, done, sems):
    experts = scratch.shape[0] // CAP
    quads = done.shape[0]
    cols = done.shape[2]
    copies = []
    for q in range(quads):
        for e in range(experts):
            scratch[pl.ds(e * CAP, CAP), :] = back_ref[e * quads + q].astype(jnp.float32)
        rows = scratch[...].astype(jnp.bfloat16)
        mixed = lax.dot_general(
            table_ref[...], jnp.concatenate([rows] * 3, axis=0), (((0,), (0,)), ((), ())),
            preferred_element_type=jnp.float32,
        )
        done[q] = mixed.astype(done.dtype)
        at = pl.ds(q * cols, cols)
        copies.append(pltpu.make_async_copy(done.at[q], mixed_hbm.at[:, at], sems.at[q]))
        copies[-1].start()
    for copy in copies:
        copy.wait()


def body(
    token_input,
    token_expert_index,
    token_request_index,
    choice_weight,
    gate_weight,
    up_weight,
    down_weight,
    adapter_first_weight,
    adapter_second_weight,
):
    experts, quads = lax.axis_size("expert"), lax.axis_size("quad")
    tokens, width = token_input.shape
    part = gate_weight.shape[2]
    cols = down_weight.shape[2]
    n_req, rank, depth = adapter_first_weight.shape[1:]
    bf16, f32 = jnp.bfloat16, jnp.float32
    dma = pltpu.SemaphoreType.DMA
    own = n_req * rank

    ids = token_expert_index.T
    weights = choice_weight.T
    outs = pl.pallas_call(
        functools.partial(pack_kernel, quads),
        out_shape=[jax.ShapeDtypeStruct((own, width // quads + depth), bf16)] * quads
        + [jax.ShapeDtypeStruct((CAP, width + LANES), bf16)] * experts,
        in_specs=[HBM] * 5,
        out_specs=[VMEM] * (quads + experts),
        scratch_shapes=[
            pltpu.VMEM(ids.shape, jnp.int32),
            pltpu.VMEM((1, tokens), jnp.int32),
            pltpu.VMEM(token_input.shape, bf16),
            pltpu.VMEM((experts * CAP, width + LANES), f32),
            dma((3 + 2 * quads,)),
        ],
        compiler_params=PARAMS,
    )(
        *in_hbm(
            ids,
            token_request_index[None],
            token_input,
            adapter_first_weight.reshape(own, depth),
            adapter_second_weight.reshape(own, width),
        )
    )
    gate2 = xor_permute(gate_weight, REQUEST, 1)
    factors, packed = outs[:quads], outs[quads:][::-1]

    blocks = [xor_permute(packed[s], "expert", s) for s in reversed(range(1, experts))]
    blocks = [packed[0]] + blocks[::-1]
    table, up = pl.pallas_call(
        stage_kernel,
        out_shape=[
            jax.ShapeDtypeStruct((3 * experts * CAP, tokens), bf16),
            jax.ShapeDtypeStruct(up_weight.shape, bf16),
        ],
        in_specs=[HBM] * 3 + [VMEM],
        out_specs=[VMEM] * 2,
        scratch_shapes=[
            pltpu.VMEM(ids.shape, jnp.int32),
            pltpu.VMEM(weights.shape, f32),
            dma((3,)),
        ],
        compiler_params=PARAMS,
    )(*in_hbm(ids, weights, up_weight), packed[0])

    factors = [factors[0]] + [xor_permute(factors[q], REQUEST, q * PAIR) for q in range(1, quads)]
    blocks, up, factors[1:] = lax.optimization_barrier((blocks[::-1], up, factors[1:]))
    blocks = blocks[::-1]
    rows = jnp.concatenate(blocks, axis=0)
    rows, up_source = lax.optimization_barrier((rows, up))
    up2 = xor_permute(up_source, REQUEST, 1)
    order, bit, slots = [0], quads // 2, []
    while bit:
        far = xor_permute(rows, REQUEST, bit * PAIR)
        order = order + [o ^ bit for o in order]
        bit //= 2
        slots = [rows, far]
        rows = jnp.concatenate(slots, axis=0) if bit else rows

    factors = jnp.concatenate(factors, axis=0)
    down = down_weight[0]
    slots, down, factors = lax.optimization_barrier((slots, down, factors))
    down2 = xor_permute(down, REQUEST, 1)
    factors = (factors, xor_permute(factors, REQUEST, 1))

    total = experts * CAP * quads
    hidden, owner = pl.pallas_call(
        functools.partial(hidden_kernel, len(slots)),
        out_shape=[
            jax.ShapeDtypeStruct((total, PAIR * part), bf16),
            jax.ShapeDtypeStruct((total, LANES), bf16),
        ],
        in_specs=[VMEM] * (len(slots) + 4),
        out_specs=[VMEM] * 2,
        compiler_params=PARAMS,
    )(*slots, gate_weight, up, gate2, up2)

    shared = [hidden] + [xor_permute(hidden, REQUEST, q * PAIR) for q in range(1, quads)]
    out = pl.pallas_call(
        functools.partial(down_kernel, order, n_req, cols),
        out_shape=jax.ShapeDtypeStruct((experts * quads, CAP, PAIR * cols), bf16),
        in_specs=[VMEM] * (quads + PAIR + 3),
        out_specs=VMEM,
        scratch_shapes=[
            pltpu.VMEM((total, depth), bf16),
            pltpu.VMEM((total, PAIR * cols), f32),
        ],
        compiler_params=PARAMS,
    )(*shared, *factors, owner, down, down2)

    back = lax.all_to_all(out, ("expert", "quad"), 0, 0, tiled=True)
    return pl.pallas_call(
        combine_kernel,
        out_shape=jax.ShapeDtypeStruct((tokens, width), bf16),
        in_specs=[VMEM] * 2,
        out_specs=HBM,
        scratch_shapes=[
            pltpu.VMEM((experts * CAP, PAIR * cols), f32),
            pltpu.VMEM((quads, tokens, PAIR * cols), bf16),
            dma((quads,)),
        ],
        compiler_params=PARAMS,
    )(table, back)


def solution(mesh):
    groups, experts, requests = mesh.devices.shape
    fine = Mesh(
        mesh.devices.reshape(groups, experts, requests // PAIR, PAIR), ("groups", "expert", *REQUEST)
    )
    everyone = P(("groups", "expert", *REQUEST), None)
    weight = P("expert", None, REQUEST)
    adapter = P(("groups", "expert"), REQUEST, None, None)
    in_specs = (everyone, everyone, P(everyone[0]), everyone) + (weight,) * 3 + (adapter,) * 2
    return jax.shard_map(body, mesh=fine, in_specs=in_specs, out_specs=everyone, check_vma=False)
```

```python
import functools

import jax
import jax.numpy as jnp
from jax import lax
from jax.experimental import pallas as pl
from jax.experimental.pallas import tpu as pltpu
from jax.sharding import Mesh, PartitionSpec as P

CAP = 4
LANES = 128
PAIR = 2
REQUEST = ("quad", "pair")
VMEM = pl.BlockSpec(memory_space=pltpu.VMEM)
HBM = pl.BlockSpec(memory_space=pltpu.HBM)
PARAMS = pltpu.CompilerParams(vmem_limit_bytes=16 * 2**20)


def xor_permute(value, axis, offset):
    return lax.ppermute(value, axis, [(i, i ^ offset) for i in range(lax.axis_size(axis))])


def slot_values(ids, values, expert):
    tokens = ids.shape[1]
    match = ids == expert
    named = jnp.sum(match.astype(jnp.float32), axis=0, keepdims=True)
    row = lax.broadcasted_iota(jnp.int32, (tokens, tokens), 0)
    col = lax.broadcasted_iota(jnp.int32, (tokens, tokens), 1)
    earlier = (row < col).astype(jnp.bfloat16)
    rank = jnp.dot(named.astype(jnp.bfloat16), earlier, preferred_element_type=jnp.float32)
    slot = lax.broadcasted_iota(jnp.int32, (CAP, tokens), 0).astype(jnp.float32)
    held = jnp.logical_and(slot == rank, named > 0)
    value = jnp.sum(jnp.where(match, values, 0.0), axis=0, keepdims=True)
    return jnp.where(held, value, 0.0)


def in_hbm(*values):
    return [pltpu.with_memory_space_constraint(v, pltpu.HBM) for v in values]


def copy_all(pairs, sems):
    copies = [pltpu.make_async_copy(a, b, sems.at[i]) for i, (a, b) in enumerate(pairs)]
    for copy in copies:
        copy.start()
    return copies


def pack_kernel(
    quads, ids_hbm, req_hbm, x_hbm, first_hbm, second_hbm, *refs
):
    factor_refs, out_refs, scratches = refs[:quads], refs[quads:-5], refs[-5:]
    ids_ref, req_ref, x_ref, scratch, sems = scratches
    half = second_hbm.shape[1] // quads
    pairs = [(ids_hbm, ids_ref), (req_hbm, req_ref), (x_hbm, x_ref)]
    for q, factor_ref in enumerate(factor_refs):
        at = pl.multiple_of((lax.axis_index("quad") ^ q) * half, half)
        pairs.append((second_hbm.at[:, pl.ds(at, half)], factor_ref.at[:, pl.ds(0, half)]))
        pairs.append((first_hbm, factor_ref.at[:, pl.ds(half, first_hbm.shape[1])]))
    copies = copy_all(pairs, sems)
    experts = len(out_refs)
    me = lax.axis_index("expert")
    width = x_ref.shape[1]
    copies[0].wait()
    copies[1].wait()
    ids = ids_ref[...]
    ones = jnp.ones(ids.shape, jnp.float32)
    table = jnp.concatenate([slot_values(ids, ones, me ^ s) for s in range(experts)], axis=0)
    owner = jnp.sum(table * (req_ref[...] + 1).astype(jnp.float32), axis=1, keepdims=True) - 1.0
    scratch[:, width:] = jnp.broadcast_to(owner, (owner.shape[0], LANES))
    copies[2].wait()
    scratch[:, :width] = jnp.dot(
        table.astype(jnp.bfloat16), x_ref[...], preferred_element_type=jnp.float32
    )
    for s, out_ref in enumerate(out_refs[::-1]):
        out_ref[...] = scratch[pl.ds(s * CAP, CAP), :].astype(out_ref.dtype)
    for copy in copies[3:]:
        copy.wait()


def stage_kernel(
    ids_hbm, weight_hbm, up_hbm, after_ref, table_ref, up_ref, ids_ref, weight_ref, sems
):
    pairs = [(ids_hbm, ids_ref), (weight_hbm, weight_ref), (up_hbm, up_ref)]
    copies = copy_all(pairs, sems)
    copies[0].wait()
    copies[1].wait()
    ids, weights = ids_ref[...], weight_ref[...]
    experts = table_ref.shape[0] // (3 * CAP)
    table = jnp.concatenate([slot_values(ids, weights, e) for e in range(experts)], axis=0)
    high = table.astype(jnp.bfloat16)
    rest = table - high.astype(jnp.float32)
    middle = rest.astype(jnp.bfloat16)
    low = (rest - middle.astype(jnp.float32)).astype(jnp.bfloat16)
    table_ref[...] = jnp.concatenate([low, middle, high], axis=0)
    for copy in copies[2:]:
        copy.wait()


def hidden_kernel(pieces, *refs):
    slot_refs, refs = refs[:pieces], refs[pieces:]
    gate_ref, up_ref, gate2_ref, up2_ref, hidden_ref, owner_ref = refs
    width, part = gate_ref.shape[1:]
    slots = jnp.concatenate([ref[...].astype(jnp.float32) for ref in slot_refs], axis=0)
    rows = slots[:, :width].astype(jnp.bfloat16)
    owner_ref[...] = slots[:, width:].astype(owner_ref.dtype)
    for b, (g_ref, u_ref) in enumerate(((gate_ref, up_ref), (gate2_ref, up2_ref))):
        gate = jnp.dot(rows, g_ref[0], preferred_element_type=jnp.float32)
        up = jnp.dot(rows, u_ref[0], preferred_element_type=jnp.float32)
        hidden = gate / (1.0 + jnp.exp(-gate)) * up
        hidden_ref[:, b * part : (b + 1) * part] = hidden.astype(hidden_ref.dtype)


def down_kernel(order, n_req, cols, *refs):
    quads = len(order)
    hid_refs, factor_refs = refs[:quads], refs[quads : quads + PAIR]
    owner_ref, own_ref, peer_ref, out_ref, whole, scratch = refs[quads + PAIR :]
    me_e, me_q, me_p = (lax.axis_index(a) for a in ("expert", "quad", "pair"))
    me_r = me_q * PAIR + me_p
    total, depth = whole.shape
    block = total // quads
    part = hid_refs[0].shape[1] // PAIR
    for q, hid_ref in enumerate(hid_refs):
        picks = [order.index(o ^ q) for o in order]
        hid = jnp.concatenate([hid_ref[j * block : (j + 1) * block, :] for j in picks], axis=0)
        for b in range(PAIR):
            at = pl.multiple_of((me_r ^ (q * PAIR + b)) * part, part)
            whole[:, pl.ds(at, part)] = hid[:, b * part : (b + 1) * part]
    hidden = whole[...]
    owner = owner_ref[:, :1].astype(jnp.int32)
    per_dev = factor_refs[0].shape[0] // quads
    rank = per_dev // n_req
    lane = lax.broadcasted_iota(jnp.int32, (1, per_dev * quads * PAIR), 1)
    first = jnp.concatenate([ref[:, PAIR * cols :] for ref in factor_refs], axis=0)
    low = lax.dot_general(
        hidden, first, (((1,), (1,)), ((), ())), preferred_element_type=jnp.float32
    )
    holder = jnp.zeros_like(lane)
    for i in range(quads * PAIR):
        holder_r = me_r ^ (i % quads * PAIR + i // quads)
        mine = holder_r * n_req + (lane - i * per_dev) // rank
        holder = jnp.where(lane // per_dev == i, mine, holder)
    chosen = jnp.where(holder == owner, low, 0.0).astype(jnp.bfloat16)
    for b, ref in enumerate((own_ref, peer_ref)):
        at = pl.ds(pl.multiple_of((me_p ^ b) * cols, cols), cols)
        second = jnp.concatenate([f[:, at] for f in factor_refs], axis=0)
        scratch[:, at] = jnp.dot(
            hidden, ref[...], preferred_element_type=jnp.float32
        ) + jnp.dot(chosen, second, preferred_element_type=jnp.float32)
    experts = block // CAP
    for i, o in enumerate(order):
        for s in range(experts):
            target = (me_e ^ s) * quads + (me_q ^ o)
            rows = scratch[pl.ds(i * block + s * CAP, CAP), :]
            out_ref[target] = rows.astype(out_ref.dtype)


def combine_kernel(table_ref, back_ref, mixed_hbm, scratch, done, sems):
    experts = scratch.shape[0] // CAP
    quads = done.shape[0]
    cols = done.shape[2]
    copies = []
    for q in range(quads):
        for e in range(experts):
            scratch[pl.ds(e * CAP, CAP), :] = back_ref[e * quads + q].astype(jnp.float32)
        rows = scratch[...].astype(jnp.bfloat16)
        mixed = lax.dot_general(
            table_ref[...], jnp.concatenate([rows] * 3, axis=0), (((0,), (0,)), ((), ())),
            preferred_element_type=jnp.float32,
        )
        done[q] = mixed.astype(done.dtype)
        at = pl.ds(q * cols, cols)
        copies.append(pltpu.make_async_copy(done.at[q], mixed_hbm.at[:, at], sems.at[q]))
        copies[-1].start()
    for copy in copies:
        copy.wait()


def body(
    token_input,
    token_expert_index,
    token_request_index,
    choice_weight,
    gate_weight,
    up_weight,
    down_weight,
    adapter_first_weight,
    adapter_second_weight,
):
    experts, quads = lax.axis_size("expert"), lax.axis_size("quad")
    tokens, width = token_input.shape
    part = gate_weight.shape[2]
    cols = down_weight.shape[2]
    n_req, rank, depth = adapter_first_weight.shape[1:]
    bf16, f32 = jnp.bfloat16, jnp.float32
    dma = pltpu.SemaphoreType.DMA
    own = n_req * rank

    ids = token_expert_index.T
    weights = choice_weight.T
    outs = pl.pallas_call(
        functools.partial(pack_kernel, quads),
        out_shape=[jax.ShapeDtypeStruct((own, width // quads + depth), bf16)] * quads
        + [jax.ShapeDtypeStruct((CAP, width + LANES), bf16)] * experts,
        in_specs=[HBM] * 5,
        out_specs=[VMEM] * (quads + experts),
        scratch_shapes=[
            pltpu.VMEM(ids.shape, jnp.int32),
            pltpu.VMEM((1, tokens), jnp.int32),
            pltpu.VMEM(token_input.shape, bf16),
            pltpu.VMEM((experts * CAP, width + LANES), f32),
            dma((3 + 2 * quads,)),
        ],
        compiler_params=PARAMS,
    )(
        *in_hbm(
            ids,
            token_request_index[None],
            token_input,
            adapter_first_weight.reshape(own, depth),
            adapter_second_weight.reshape(own, width),
        )
    )
    gate2 = xor_permute(gate_weight, REQUEST, 1)
    factors, packed = outs[:quads], outs[quads:][::-1]

    blocks = [xor_permute(packed[s], "expert", s) for s in reversed(range(1, experts))]
    blocks = [packed[0]] + blocks[::-1]
    table, up = pl.pallas_call(
        stage_kernel,
        out_shape=[
            jax.ShapeDtypeStruct((3 * experts * CAP, tokens), bf16),
            jax.ShapeDtypeStruct(up_weight.shape, bf16),
        ],
        in_specs=[HBM] * 3 + [VMEM],
        out_specs=[VMEM] * 2,
        scratch_shapes=[
            pltpu.VMEM(ids.shape, jnp.int32),
            pltpu.VMEM(weights.shape, f32),
            dma((3,)),
        ],
        compiler_params=PARAMS,
    )(*in_hbm(ids, weights, up_weight), packed[0])

    factors = [factors[0]] + [xor_permute(factors[q], REQUEST, q * PAIR) for q in range(1, quads)]
    far_first = sorted(range(1, experts), key=lambda s: (s == 1, s))
    tied, up, factors[1:] = lax.optimization_barrier(
        ([blocks[s] for s in far_first], up, factors[1:])
    )
    blocks = [blocks[0]] + [tied[far_first.index(s)] for s in range(1, experts)]
    rows = jnp.concatenate(blocks, axis=0)
    rows, up_source = lax.optimization_barrier((rows, up))
    up2 = xor_permute(up_source, REQUEST, 1)
    order, bit, slots = [0], quads // 2, []
    while bit:
        far = xor_permute(rows, REQUEST, bit * PAIR)
        order = order + [o ^ bit for o in order]
        bit //= 2
        slots = [rows, far]
        rows = jnp.concatenate(slots, axis=0) if bit else rows

    factors = jnp.concatenate(factors, axis=0)
    down = down_weight[0]
    slots, down, factors = lax.optimization_barrier((slots, down, factors))
    down2 = xor_permute(down, REQUEST, 1)
    factors = (factors, xor_permute(factors, REQUEST, 1))

    total = experts * CAP * quads
    hidden, owner = pl.pallas_call(
        functools.partial(hidden_kernel, len(slots)),
        out_shape=[
            jax.ShapeDtypeStruct((total, PAIR * part), bf16),
            jax.ShapeDtypeStruct((total, LANES), bf16),
        ],
        in_specs=[VMEM] * (len(slots) + 4),
        out_specs=[VMEM] * 2,
        compiler_params=PARAMS,
    )(*slots, gate_weight, up, gate2, up2)

    shared = [hidden] + [xor_permute(hidden, REQUEST, q * PAIR) for q in range(1, quads)]
    out = pl.pallas_call(
        functools.partial(down_kernel, order, n_req, cols),
        out_shape=jax.ShapeDtypeStruct((experts * quads, CAP, PAIR * cols), bf16),
        in_specs=[VMEM] * (quads + PAIR + 3),
        out_specs=VMEM,
        scratch_shapes=[
            pltpu.VMEM((total, depth), bf16),
            pltpu.VMEM((total, PAIR * cols), f32),
        ],
        compiler_params=PARAMS,
    )(*shared, *factors, owner, down, down2)

    back = lax.all_to_all(out, ("expert", "quad"), 0, 0, tiled=True)
    return pl.pallas_call(
        combine_kernel,
        out_shape=jax.ShapeDtypeStruct((tokens, width), bf16),
        in_specs=[VMEM] * 2,
        out_specs=HBM,
        scratch_shapes=[
            pltpu.VMEM((experts * CAP, PAIR * cols), f32),
            pltpu.VMEM((quads, tokens, PAIR * cols), bf16),
            dma((quads,)),
        ],
        compiler_params=PARAMS,
    )(table, back)


def solution(mesh):
    groups, experts, requests = mesh.devices.shape
    fine = Mesh(
        mesh.devices.reshape(groups, experts, requests // PAIR, PAIR), ("groups", "expert", *REQUEST)
    )
    everyone = P(("groups", "expert", *REQUEST), None)
    weight = P("expert", None, REQUEST)
    adapter = P(("groups", "expert"), REQUEST, None, None)
    in_specs = (everyone, everyone, P(everyone[0]), everyone) + (weight,) * 3 + (adapter,) * 2
    return jax.shard_map(body, mesh=fine, in_specs=in_specs, out_specs=everyone, check_vma=False)
```

```python
import functools

import jax
import jax.numpy as jnp
from jax import lax
from jax.experimental import pallas as pl
from jax.experimental.pallas import tpu as pltpu
from jax.sharding import Mesh, PartitionSpec as P

CAP = 4
LANES = 128
PAIR = 2
REQUEST = ("quad", "pair")
VMEM = pl.BlockSpec(memory_space=pltpu.VMEM)
HBM = pl.BlockSpec(memory_space=pltpu.HBM)
PARAMS = pltpu.CompilerParams(vmem_limit_bytes=16 * 2**20)


def xor_permute(value, axis, offset):
    return lax.ppermute(value, axis, [(i, i ^ offset) for i in range(lax.axis_size(axis))])


def slot_values(ids, values, expert):
    tokens = ids.shape[1]
    match = ids == expert
    named = jnp.sum(match.astype(jnp.float32), axis=0, keepdims=True)
    row = lax.broadcasted_iota(jnp.int32, (tokens, tokens), 0)
    col = lax.broadcasted_iota(jnp.int32, (tokens, tokens), 1)
    earlier = (row < col).astype(jnp.bfloat16)
    rank = jnp.dot(named.astype(jnp.bfloat16), earlier, preferred_element_type=jnp.float32)
    slot = lax.broadcasted_iota(jnp.int32, (CAP, tokens), 0).astype(jnp.float32)
    held = jnp.logical_and(slot == rank, named > 0)
    value = jnp.sum(jnp.where(match, values, 0.0), axis=0, keepdims=True)
    return jnp.where(held, value, 0.0)


def in_hbm(*values):
    return [pltpu.with_memory_space_constraint(v, pltpu.HBM) for v in values]


def copy_all(pairs, sems):
    copies = [pltpu.make_async_copy(a, b, sems.at[i]) for i, (a, b) in enumerate(pairs)]
    for copy in copies:
        copy.start()
    return copies


def pack_kernel(
    quads, ids_hbm, req_hbm, x_hbm, first_hbm, second_hbm, *refs
):
    factor_refs, out_refs, scratches = refs[:quads], refs[quads:-5], refs[-5:]
    ids_ref, req_ref, x_ref, scratch, sems = scratches
    half = second_hbm.shape[1] // quads
    pairs = [(ids_hbm, ids_ref), (req_hbm, req_ref)]
    parts = [pl.ds(i * half, half) for i in range(quads)]
    pairs += [(x_hbm.at[:, at], x_ref.at[:, at]) for at in parts]
    for q, factor_ref in enumerate(factor_refs):
        at = pl.multiple_of((lax.axis_index("quad") ^ q) * half, half)
        pairs.append((second_hbm.at[:, pl.ds(at, half)], factor_ref.at[:, pl.ds(0, half)]))
        pairs.append((first_hbm, factor_ref.at[:, pl.ds(half, first_hbm.shape[1])]))
    copies = copy_all(pairs, sems)
    experts = len(out_refs)
    me = lax.axis_index("expert")
    width = x_ref.shape[1]
    copies[0].wait()
    copies[1].wait()
    ids = ids_ref[...]
    ones = jnp.ones(ids.shape, jnp.float32)
    table = jnp.concatenate([slot_values(ids, ones, me ^ s) for s in range(experts)], axis=0)
    owner = jnp.sum(table * (req_ref[...] + 1).astype(jnp.float32), axis=1, keepdims=True) - 1.0
    scratch[:, width:] = jnp.broadcast_to(owner, (owner.shape[0], LANES))
    table = table.astype(jnp.bfloat16)
    for copy, at in zip(copies[2:], parts):
        copy.wait()
        scratch[:, at] = jnp.dot(table, x_ref[:, at], preferred_element_type=jnp.float32)
    for s, out_ref in enumerate(out_refs[::-1]):
        out_ref[...] = scratch[pl.ds(s * CAP, CAP), :].astype(out_ref.dtype)
    for copy in copies[2 + quads :]:
        copy.wait()


def stage_kernel(
    ids_hbm, weight_hbm, up_hbm, after_ref, table_ref, up_ref, ids_ref, weight_ref, sems
):
    pairs = [(ids_hbm, ids_ref), (weight_hbm, weight_ref), (up_hbm, up_ref)]
    copies = copy_all(pairs, sems)
    copies[0].wait()
    copies[1].wait()
    ids, weights = ids_ref[...], weight_ref[...]
    experts = table_ref.shape[0] // (3 * CAP)
    table = jnp.concatenate([slot_values(ids, weights, e) for e in range(experts)], axis=0)
    high = table.astype(jnp.bfloat16)
    rest = table - high.astype(jnp.float32)
    middle = rest.astype(jnp.bfloat16)
    low = (rest - middle.astype(jnp.float32)).astype(jnp.bfloat16)
    table_ref[...] = jnp.concatenate([low, middle, high], axis=0)
    for copy in copies[2:]:
        copy.wait()


def hidden_kernel(pieces, *refs):
    slot_refs, refs = refs[:pieces], refs[pieces:]
    gate_ref, up_ref, gate2_ref, up2_ref, hidden_ref, owner_ref = refs
    width, part = gate_ref.shape[1:]
    slots = jnp.concatenate([ref[...].astype(jnp.float32) for ref in slot_refs], axis=0)
    rows = slots[:, :width].astype(jnp.bfloat16)
    owner_ref[...] = slots[:, width:].astype(owner_ref.dtype)
    for b, (g_ref, u_ref) in enumerate(((gate_ref, up_ref), (gate2_ref, up2_ref))):
        gate = jnp.dot(rows, g_ref[0], preferred_element_type=jnp.float32)
        up = jnp.dot(rows, u_ref[0], preferred_element_type=jnp.float32)
        hidden = gate / (1.0 + jnp.exp(-gate)) * up
        hidden_ref[:, b * part : (b + 1) * part] = hidden.astype(hidden_ref.dtype)


def down_kernel(order, n_req, cols, *refs):
    quads = len(order)
    hid_refs, factor_refs = refs[:quads], refs[quads : quads + PAIR]
    owner_ref, own_ref, peer_ref, out_ref, whole, scratch = refs[quads + PAIR :]
    me_e, me_q, me_p = (lax.axis_index(a) for a in ("expert", "quad", "pair"))
    me_r = me_q * PAIR + me_p
    total, depth = whole.shape
    block = total // quads
    part = hid_refs[0].shape[1] // PAIR
    for q, hid_ref in enumerate(hid_refs):
        picks = [order.index(o ^ q) for o in order]
        hid = jnp.concatenate([hid_ref[j * block : (j + 1) * block, :] for j in picks], axis=0)
        for b in range(PAIR):
            at = pl.multiple_of((me_r ^ (q * PAIR + b)) * part, part)
            whole[:, pl.ds(at, part)] = hid[:, b * part : (b + 1) * part]
    hidden = whole[...]
    owner = owner_ref[:, :1].astype(jnp.int32)
    per_dev = factor_refs[0].shape[0] // quads
    rank = per_dev // n_req
    lane = lax.broadcasted_iota(jnp.int32, (1, per_dev * quads * PAIR), 1)
    first = jnp.concatenate([ref[:, PAIR * cols :] for ref in factor_refs], axis=0)
    low = lax.dot_general(
        hidden, first, (((1,), (1,)), ((), ())), preferred_element_type=jnp.float32
    )
    holder = jnp.zeros_like(lane)
    for i in range(quads * PAIR):
        holder_r = me_r ^ (i % quads * PAIR + i // quads)
        mine = holder_r * n_req + (lane - i * per_dev) // rank
        holder = jnp.where(lane // per_dev == i, mine, holder)
    chosen = jnp.where(holder == owner, low, 0.0).astype(jnp.bfloat16)
    for b, ref in enumerate((own_ref, peer_ref)):
        at = pl.ds(pl.multiple_of((me_p ^ b) * cols, cols), cols)
        second = jnp.concatenate([f[:, at] for f in factor_refs], axis=0)
        scratch[:, at] = jnp.dot(
            hidden, ref[...], preferred_element_type=jnp.float32
        ) + jnp.dot(chosen, second, preferred_element_type=jnp.float32)
    experts = block // CAP
    for i, o in enumerate(order):
        for s in range(experts):
            target = (me_e ^ s) * quads + (me_q ^ o)
            rows = scratch[pl.ds(i * block + s * CAP, CAP), :]
            out_ref[target] = rows.astype(out_ref.dtype)


def combine_kernel(table_ref, back_ref, mixed_hbm, scratch, done, sems):
    experts = scratch.shape[0] // CAP
    chunks, _, size = done.shape
    quads = back_ref.shape[0] // experts
    each = chunks // quads
    copies = []
    for i in range(chunks):
        q, lanes = i // each, pl.ds(i % each * size, size)
        for e in range(experts):
            scratch[pl.ds(e * CAP, CAP), lanes] = back_ref[e * quads + q, :, lanes].astype(jnp.float32)
        rows = scratch[:, lanes].astype(jnp.bfloat16)
        mixed = lax.dot_general(
            table_ref[...], jnp.concatenate([rows] * 3, axis=0), (((0,), (0,)), ((), ())),
            preferred_element_type=jnp.float32,
        )
        done[i] = mixed.astype(done.dtype)
        at = pl.ds(i * size, size)
        copies.append(pltpu.make_async_copy(done.at[i], mixed_hbm.at[:, at], sems.at[i]))
        copies[-1].start()
    for copy in copies:
        copy.wait()


def body(
    token_input,
    token_expert_index,
    token_request_index,
    choice_weight,
    gate_weight,
    up_weight,
    down_weight,
    adapter_first_weight,
    adapter_second_weight,
):
    experts, quads = lax.axis_size("expert"), lax.axis_size("quad")
    tokens, width = token_input.shape
    part = gate_weight.shape[2]
    cols = down_weight.shape[2]
    n_req, rank, depth = adapter_first_weight.shape[1:]
    bf16, f32 = jnp.bfloat16, jnp.float32
    dma = pltpu.SemaphoreType.DMA
    own = n_req * rank

    ids = token_expert_index.T
    weights = choice_weight.T
    outs = pl.pallas_call(
        functools.partial(pack_kernel, quads),
        out_shape=[jax.ShapeDtypeStruct((own, width // quads + depth), bf16)] * quads
        + [jax.ShapeDtypeStruct((CAP, width + LANES), bf16)] * experts,
        in_specs=[HBM] * 5,
        out_specs=[VMEM] * (quads + experts),
        scratch_shapes=[
            pltpu.VMEM(ids.shape, jnp.int32),
            pltpu.VMEM((1, tokens), jnp.int32),
            pltpu.VMEM(token_input.shape, bf16),
            pltpu.VMEM((experts * CAP, width + LANES), f32),
            dma((2 + 3 * quads,)),
        ],
        compiler_params=PARAMS,
    )(
        *in_hbm(
            ids,
            token_request_index[None],
            token_input,
            adapter_first_weight.reshape(own, depth),
            adapter_second_weight.reshape(own, width),
        )
    )
    gate2 = xor_permute(gate_weight, REQUEST, 1)
    factors, packed = outs[:quads], outs[quads:][::-1]

    blocks = [xor_permute(packed[s], "expert", s) for s in reversed(range(1, experts))]
    blocks = [packed[0]] + blocks[::-1]
    table, up = pl.pallas_call(
        stage_kernel,
        out_shape=[
            jax.ShapeDtypeStruct((3 * experts * CAP, tokens), bf16),
            jax.ShapeDtypeStruct(up_weight.shape, bf16),
        ],
        in_specs=[HBM] * 3 + [VMEM],
        out_specs=[VMEM] * 2,
        scratch_shapes=[
            pltpu.VMEM(ids.shape, jnp.int32),
            pltpu.VMEM(weights.shape, f32),
            dma((3,)),
        ],
        compiler_params=PARAMS,
    )(*in_hbm(ids, weights, up_weight), packed[0])

    factors = [factors[0]] + [xor_permute(factors[q], REQUEST, q * PAIR) for q in range(1, quads)]
    far_first = sorted(range(1, experts), key=lambda s: (s == 1, s))
    tied, up, factors[1:] = lax.optimization_barrier(
        ([blocks[s] for s in far_first], up, factors[1:])
    )
    blocks = [blocks[0]] + [tied[far_first.index(s)] for s in range(1, experts)]
    rows = jnp.concatenate(blocks, axis=0)
    rows, up_source = lax.optimization_barrier((rows, up))
    up2 = xor_permute(up_source, REQUEST, 1)
    order, bit, slots = [0], quads // 2, []
    while bit:
        far = xor_permute(rows, REQUEST, bit * PAIR)
        order = order + [o ^ bit for o in order]
        bit //= 2
        slots = [rows, far]
        rows = jnp.concatenate(slots, axis=0) if bit else rows

    factors = jnp.concatenate(factors, axis=0)
    down = down_weight[0]
    slots, down, factors = lax.optimization_barrier((slots, down, factors))
    down2 = xor_permute(down, REQUEST, 1)
    factors = (factors, xor_permute(factors, REQUEST, 1))

    total = experts * CAP * quads
    hidden, owner = pl.pallas_call(
        functools.partial(hidden_kernel, len(slots)),
        out_shape=[
            jax.ShapeDtypeStruct((total, PAIR * part), bf16),
            jax.ShapeDtypeStruct((total, LANES), bf16),
        ],
        in_specs=[VMEM] * (len(slots) + 4),
        out_specs=[VMEM] * 2,
        compiler_params=PARAMS,
    )(*slots, gate_weight, up, gate2, up2)

    shared = [hidden] + [xor_permute(hidden, REQUEST, q * PAIR) for q in range(1, quads)]
    out = pl.pallas_call(
        functools.partial(down_kernel, order, n_req, cols),
        out_shape=jax.ShapeDtypeStruct((experts * quads, CAP, PAIR * cols), bf16),
        in_specs=[VMEM] * (quads + PAIR + 3),
        out_specs=VMEM,
        scratch_shapes=[
            pltpu.VMEM((total, depth), bf16),
            pltpu.VMEM((total, PAIR * cols), f32),
        ],
        compiler_params=PARAMS,
    )(*shared, *factors, owner, down, down2)

    back = lax.all_to_all(out, ("expert", "quad"), 0, 0, tiled=True)
    return pl.pallas_call(
        combine_kernel,
        out_shape=jax.ShapeDtypeStruct((tokens, width), bf16),
        in_specs=[VMEM] * 2,
        out_specs=HBM,
        scratch_shapes=[
            pltpu.VMEM((experts * CAP, PAIR * cols), f32),
            pltpu.VMEM((PAIR * quads, tokens, cols), bf16),
            dma((PAIR * quads,)),
        ],
        compiler_params=PARAMS,
    )(table, back)


def solution(mesh):
    groups, experts, requests = mesh.devices.shape
    fine = Mesh(
        mesh.devices.reshape(groups, experts, requests // PAIR, PAIR), ("groups", "expert", *REQUEST)
    )
    everyone = P(("groups", "expert", *REQUEST), None)
    weight = P("expert", None, REQUEST)
    adapter = P(("groups", "expert"), REQUEST, None, None)
    in_specs = (everyone, everyone, P(everyone[0]), everyone) + (weight,) * 3 + (adapter,) * 2
    return jax.shard_map(body, mesh=fine, in_specs=in_specs, out_specs=everyone, check_vma=False)
```

```python
import functools

import jax
import jax.numpy as jnp
from jax import lax
from jax.experimental import pallas as pl
from jax.experimental.pallas import tpu as pltpu
from jax.sharding import Mesh, PartitionSpec as P

CAP = 4
LANES = 128
PAIR = 2
REQUEST = ("quad", "pair")
VMEM = pl.BlockSpec(memory_space=pltpu.VMEM)
HBM = pl.BlockSpec(memory_space=pltpu.HBM)
PARAMS = pltpu.CompilerParams(vmem_limit_bytes=16 * 2**20)


def xor_permute(value, axis, offset):
    return lax.ppermute(value, axis, [(i, i ^ offset) for i in range(lax.axis_size(axis))])


def slot_values(ids, values, expert):
    tokens = ids.shape[1]
    match = ids == expert
    named = jnp.sum(match.astype(jnp.float32), axis=0, keepdims=True)
    row = lax.broadcasted_iota(jnp.int32, (tokens, tokens), 0)
    col = lax.broadcasted_iota(jnp.int32, (tokens, tokens), 1)
    earlier = (row < col).astype(jnp.bfloat16)
    rank = jnp.dot(named.astype(jnp.bfloat16), earlier, preferred_element_type=jnp.float32)
    slot = lax.broadcasted_iota(jnp.int32, (CAP, tokens), 0).astype(jnp.float32)
    held = jnp.logical_and(slot == rank, named > 0)
    value = jnp.sum(jnp.where(match, values, 0.0), axis=0, keepdims=True)
    return jnp.where(held, value, 0.0)


def in_hbm(*values):
    return [pltpu.with_memory_space_constraint(v, pltpu.HBM) for v in values]


def copy_all(pairs, sems):
    copies = [pltpu.make_async_copy(a, b, sems.at[i]) for i, (a, b) in enumerate(pairs)]
    for copy in copies:
        copy.start()
    return copies


def pack_kernel(
    quads, ids_hbm, req_hbm, x_hbm, first_hbm, second_hbm, *refs
):
    factor_refs, out_refs, scratches = refs[:quads], refs[quads:-6], refs[-6:]
    ids_ref, req_ref, x_ref, scratch, folded, sems = scratches
    half = second_hbm.shape[1] // quads
    pairs = [(ids_hbm, ids_ref), (req_hbm, req_ref), (x_hbm, x_ref)]
    for q, factor_ref in enumerate(factor_refs):
        at = pl.multiple_of((lax.axis_index("quad") ^ q) * half, half)
        pairs.append((second_hbm.at[:, pl.ds(at, half)], factor_ref.at[:, pl.ds(0, half)]))
        pairs.append((first_hbm, factor_ref.at[:, pl.ds(half, first_hbm.shape[1])]))
    copies = copy_all(pairs, sems)
    experts = len(out_refs)
    me = lax.axis_index("expert")
    width = x_ref.shape[1]
    copies[0].wait()
    copies[1].wait()
    ids = ids_ref[...]
    ones = jnp.ones(ids.shape, jnp.float32)
    table = jnp.concatenate([slot_values(ids, ones, me ^ s) for s in range(experts)], axis=0)
    owner = jnp.sum(table * (req_ref[...] + 1).astype(jnp.float32), axis=1, keepdims=True) - 1.0
    scratch[:, width:] = jnp.broadcast_to(owner, (owner.shape[0], LANES))
    copies[2].wait()
    scratch[:, :width] = jnp.dot(
        table.astype(jnp.bfloat16), x_ref[...], preferred_element_type=jnp.float32
    )
    start = half + first_hbm.shape[1]
    lanes = factor_refs[0].shape[1] - start
    full = scratch.shape[1]
    folded[...] = jnp.zeros_like(folded)
    for i in range(-(-full // lanes)):
        size = min(lanes, full - i * lanes)
        folded[pl.ds(i * CAP, CAP), :size] = scratch[:CAP, i * lanes : i * lanes + size]
    for factor_ref in factor_refs:
        factor_ref[:, start:] = folded[...].astype(factor_ref.dtype)
    for s, out_ref in enumerate(out_refs[::-1]):
        out_ref[...] = scratch[pl.ds(s * CAP, CAP), :].astype(out_ref.dtype)
    for copy in copies[3:]:
        copy.wait()


def stage_kernel(
    ids_hbm, weight_hbm, up_hbm, after_ref, table_ref, up_ref, ids_ref, weight_ref, sems
):
    pairs = [(ids_hbm, ids_ref), (weight_hbm, weight_ref), (up_hbm, up_ref)]
    copies = copy_all(pairs, sems)
    copies[0].wait()
    copies[1].wait()
    ids, weights = ids_ref[...], weight_ref[...]
    experts = table_ref.shape[0] // (3 * CAP)
    table = jnp.concatenate([slot_values(ids, weights, e) for e in range(experts)], axis=0)
    high = table.astype(jnp.bfloat16)
    rest = table - high.astype(jnp.float32)
    middle = rest.astype(jnp.bfloat16)
    low = (rest - middle.astype(jnp.float32)).astype(jnp.bfloat16)
    table_ref[...] = jnp.concatenate([low, middle, high], axis=0)
    for copy in copies[2:]:
        copy.wait()


def hidden_kernel(order, start, *refs):
    quads = len(order)
    own_ref, folded_refs, refs = refs[0], refs[1:quads], refs[quads:]
    slot_refs, refs = refs[:2], refs[2:]
    gate_ref, up_ref, gate2_ref, up2_ref, hidden_ref, owner_ref, slots, folded = refs
    width, part = gate_ref.shape[1:]
    full = slots.shape[1]
    block = slots.shape[0] // quads
    rest = block - CAP
    pieces = [ref[...].astype(jnp.float32) for ref in slot_refs]
    held = pieces[0].shape[0] // rest
    for i, o in enumerate(order):
        at = (i % held) * rest
        slots[pl.ds(i * block + CAP, rest), :] = pieces[i // held][at : at + rest, :]
        if o == 0:
            slots[pl.ds(i * block, CAP), :] = own_ref[...].astype(jnp.float32)
            continue
        folded[...] = folded_refs[o - 1][:, start:].astype(jnp.float32)
        lanes = folded.shape[1]
        for k in range(-(-full // lanes)):
            size = min(lanes, full - k * lanes)
            slots[pl.ds(i * block, CAP), k * lanes : k * lanes + size] = folded[
                pl.ds(k * CAP, CAP), :size
            ]
    rows = slots[:, :width].astype(jnp.bfloat16)
    owner_ref[...] = slots[:, width:].astype(owner_ref.dtype)
    for b, (g_ref, u_ref) in enumerate(((gate_ref, up_ref), (gate2_ref, up2_ref))):
        gate = jnp.dot(rows, g_ref[0], preferred_element_type=jnp.float32)
        up = jnp.dot(rows, u_ref[0], preferred_element_type=jnp.float32)
        hidden = gate / (1.0 + jnp.exp(-gate)) * up
        hidden_ref[:, b * part : (b + 1) * part] = hidden.astype(hidden_ref.dtype)


def down_kernel(order, n_req, cols, *refs):
    quads = len(order)
    hid_refs, factor_refs = refs[:quads], refs[quads : quads + PAIR]
    owner_ref, own_ref, peer_ref, out_ref, whole, scratch = refs[quads + PAIR :]
    me_e, me_q, me_p = (lax.axis_index(a) for a in ("expert", "quad", "pair"))
    me_r = me_q * PAIR + me_p
    total, depth = whole.shape
    block = total // quads
    part = hid_refs[0].shape[1] // PAIR
    for q, hid_ref in enumerate(hid_refs):
        picks = [order.index(o ^ q) for o in order]
        hid = jnp.concatenate([hid_ref[j * block : (j + 1) * block, :] for j in picks], axis=0)
        for b in range(PAIR):
            at = pl.multiple_of((me_r ^ (q * PAIR + b)) * part, part)
            whole[:, pl.ds(at, part)] = hid[:, b * part : (b + 1) * part]
    hidden = whole[...]
    owner = owner_ref[:, :1].astype(jnp.int32)
    per_dev = factor_refs[0].shape[0] // quads
    rank = per_dev // n_req
    lane = lax.broadcasted_iota(jnp.int32, (1, per_dev * quads * PAIR), 1)
    first = jnp.concatenate(
        [ref[:, PAIR * cols : PAIR * cols + depth] for ref in factor_refs], axis=0
    )
    low = lax.dot_general(
        hidden, first, (((1,), (1,)), ((), ())), preferred_element_type=jnp.float32
    )
    holder = jnp.zeros_like(lane)
    for i in range(quads * PAIR):
        holder_r = me_r ^ (i % quads * PAIR + i // quads)
        mine = holder_r * n_req + (lane - i * per_dev) // rank
        holder = jnp.where(lane // per_dev == i, mine, holder)
    chosen = jnp.where(holder == owner, low, 0.0).astype(jnp.bfloat16)
    for b, ref in enumerate((own_ref, peer_ref)):
        at = pl.ds(pl.multiple_of((me_p ^ b) * cols, cols), cols)
        second = jnp.concatenate([f[:, at] for f in factor_refs], axis=0)
        scratch[:, at] = jnp.dot(
            hidden, ref[...], preferred_element_type=jnp.float32
        ) + jnp.dot(chosen, second, preferred_element_type=jnp.float32)
    experts = block // CAP
    for i, o in enumerate(order):
        for s in range(experts):
            target = (me_e ^ s) * quads + (me_q ^ o)
            rows = scratch[pl.ds(i * block + s * CAP, CAP), :]
            out_ref[target] = rows.astype(out_ref.dtype)


def combine_kernel(table_ref, back_ref, mixed_hbm, scratch, done, sems):
    experts = scratch.shape[0] // CAP
    quads = done.shape[0]
    cols = done.shape[2]
    copies = []
    for q in range(quads):
        for e in range(experts):
            scratch[pl.ds(e * CAP, CAP), :] = back_ref[e * quads + q].astype(jnp.float32)
        rows = scratch[...].astype(jnp.bfloat16)
        mixed = lax.dot_general(
            table_ref[...], jnp.concatenate([rows] * 3, axis=0), (((0,), (0,)), ((), ())),
            preferred_element_type=jnp.float32,
        )
        done[q] = mixed.astype(done.dtype)
        at = pl.ds(q * cols, cols)
        copies.append(pltpu.make_async_copy(done.at[q], mixed_hbm.at[:, at], sems.at[q]))
        copies[-1].start()
    for copy in copies:
        copy.wait()


def body(
    token_input,
    token_expert_index,
    token_request_index,
    choice_weight,
    gate_weight,
    up_weight,
    down_weight,
    adapter_first_weight,
    adapter_second_weight,
):
    experts, quads = lax.axis_size("expert"), lax.axis_size("quad")
    tokens, width = token_input.shape
    part = gate_weight.shape[2]
    cols = down_weight.shape[2]
    n_req, rank, depth = adapter_first_weight.shape[1:]
    bf16, f32 = jnp.bfloat16, jnp.float32
    dma = pltpu.SemaphoreType.DMA
    own = n_req * rank

    fold = -(-(width // LANES + 1) // (own // CAP)) * LANES
    ids = token_expert_index.T
    weights = choice_weight.T
    outs = pl.pallas_call(
        functools.partial(pack_kernel, quads),
        out_shape=[jax.ShapeDtypeStruct((own, width // quads + depth + fold), bf16)] * quads
        + [jax.ShapeDtypeStruct((CAP, width + LANES), bf16)] * experts,
        in_specs=[HBM] * 5,
        out_specs=[VMEM] * (quads + experts),
        scratch_shapes=[
            pltpu.VMEM(ids.shape, jnp.int32),
            pltpu.VMEM((1, tokens), jnp.int32),
            pltpu.VMEM(token_input.shape, bf16),
            pltpu.VMEM((experts * CAP, width + LANES), f32),
            pltpu.VMEM((own, fold), f32),
            dma((3 + 2 * quads,)),
        ],
        compiler_params=PARAMS,
    )(
        *in_hbm(
            ids,
            token_request_index[None],
            token_input,
            adapter_first_weight.reshape(own, depth),
            adapter_second_weight.reshape(own, width),
        )
    )
    gate2 = xor_permute(gate_weight, REQUEST, 1)
    factors, packed = outs[:quads], outs[quads:][::-1]

    blocks = [xor_permute(packed[s], "expert", s) for s in reversed(range(1, experts))]
    blocks = [packed[0]] + blocks[::-1]
    table, up = pl.pallas_call(
        stage_kernel,
        out_shape=[
            jax.ShapeDtypeStruct((3 * experts * CAP, tokens), bf16),
            jax.ShapeDtypeStruct(up_weight.shape, bf16),
        ],
        in_specs=[HBM] * 3 + [VMEM],
        out_specs=[VMEM] * 2,
        scratch_shapes=[
            pltpu.VMEM(ids.shape, jnp.int32),
            pltpu.VMEM(weights.shape, f32),
            dma((3,)),
        ],
        compiler_params=PARAMS,
    )(*in_hbm(ids, weights, up_weight), packed[0])

    factors = [factors[0]] + [xor_permute(factors[q], REQUEST, q * PAIR) for q in range(1, quads)]
    far_first = sorted(range(1, experts), key=lambda s: (s == 1, s))
    tied, up, factors[1:] = lax.optimization_barrier(
        ([blocks[s] for s in far_first], up, factors[1:])
    )
    blocks = [blocks[0]] + [tied[far_first.index(s)] for s in range(1, experts)]
    rows = jnp.concatenate(blocks[1:], axis=0)
    rows, up_source = lax.optimization_barrier((rows, up))
    up2 = xor_permute(up_source, REQUEST, 1)
    order, bit, slots = [0], quads // 2, []
    while bit:
        far = xor_permute(rows, REQUEST, bit * PAIR)
        order = order + [o ^ bit for o in order]
        bit //= 2
        slots = [rows, far]
        rows = jnp.concatenate(slots, axis=0) if bit else rows

    folded = factors[1:]
    factors = jnp.concatenate(factors, axis=0)
    down = down_weight[0]
    slots, down, factors = lax.optimization_barrier((slots, down, factors))
    down2 = xor_permute(down, REQUEST, 1)
    factors = (factors, xor_permute(factors, REQUEST, 1))

    total = experts * CAP * quads
    hidden, owner = pl.pallas_call(
        functools.partial(hidden_kernel, order, PAIR * cols + depth),
        out_shape=[
            jax.ShapeDtypeStruct((total, PAIR * part), bf16),
            jax.ShapeDtypeStruct((total, LANES), bf16),
        ],
        in_specs=[VMEM] * (quads + 6),
        out_specs=[VMEM] * 2,
        scratch_shapes=[pltpu.VMEM((total, width + LANES), f32), pltpu.VMEM((own, fold), f32)],
        compiler_params=PARAMS,
    )(blocks[0], *folded, *slots, gate_weight, up, gate2, up2)

    shared = [hidden] + [xor_permute(hidden, REQUEST, q * PAIR) for q in range(1, quads)]
    out = pl.pallas_call(
        functools.partial(down_kernel, order, n_req, cols),
        out_shape=jax.ShapeDtypeStruct((experts * quads, CAP, PAIR * cols), bf16),
        in_specs=[VMEM] * (quads + PAIR + 3),
        out_specs=VMEM,
        scratch_shapes=[
            pltpu.VMEM((total, depth), bf16),
            pltpu.VMEM((total, PAIR * cols), f32),
        ],
        compiler_params=PARAMS,
    )(*shared, *factors, owner, down, down2)

    back = lax.all_to_all(out, ("expert", "quad"), 0, 0, tiled=True)
    return pl.pallas_call(
        combine_kernel,
        out_shape=jax.ShapeDtypeStruct((tokens, width), bf16),
        in_specs=[VMEM] * 2,
        out_specs=HBM,
        scratch_shapes=[
            pltpu.VMEM((experts * CAP, PAIR * cols), f32),
            pltpu.VMEM((quads, tokens, PAIR * cols), bf16),
            dma((quads,)),
        ],
        compiler_params=PARAMS,
    )(table, back)


def solution(mesh):
    groups, experts, requests = mesh.devices.shape
    fine = Mesh(
        mesh.devices.reshape(groups, experts, requests // PAIR, PAIR), ("groups", "expert", *REQUEST)
    )
    everyone = P(("groups", "expert", *REQUEST), None)
    weight = P("expert", None, REQUEST)
    adapter = P(("groups", "expert"), REQUEST, None, None)
    in_specs = (everyone, everyone, P(everyone[0]), everyone) + (weight,) * 3 + (adapter,) * 2
    return jax.shard_map(body, mesh=fine, in_specs=in_specs, out_specs=everyone, check_vma=False)
```
